32 devices in a mesh: tm: 2 (over core), height: 4 (over y, x), chan: 4 (over z).
Axes of the slice: x: 2, y: 2, z: 4, core: 2. Of those that a mesh axis runs over, the one named last changes fastest.
Arguments:
- frames: bfloat16 [4, 16, 256, 128], P('tm', 'height', 'chan'), may hold values from -6 to 6
- grad_out: bfloat16 [4, 16, 256, 128], P('tm', 'height', 'chan'), may hold values from -6 to 6
- weight_one: bfloat16 [256, 3, 3, 3, 256], P('chan'), may hold values from -0.078125 to 0.078125
- weight_two: bfloat16 [256, 3, 3, 3, 256], P('chan'), may hold values from -0.078125 to 0.078125
Outputs:
- grad_frames: bfloat16 [4, 16, 256, 128], P('tm', 'height', 'chan')
- grad_one: float32 [256, 3, 3, 3, 256], P('chan')
- grad_two: float32 [256, 3, 3, 3, 256], P('chan')
The draws below stay inside these ranges and needn't reach their ends.
All inputs are finite; a program needn't handle non-finite values.
Results may differ from the reference program's by a relative error of at most 0.015.
Values may be sent and summed in bfloat16 or wider, within the bound.
A program may use at most 128 MiB of HBM per device.

```python
import jax
import jax.numpy as jnp
from jax import lax

CHANNELS = 256
COLS = 128
FRAMES = 4
HEIGHT_ROWS = 16


def levels(rng, shape, cuts, smallest, top_value):
    loudness, own = 1.0, jax.random.fold_in(rng, 6)
    for axis_at, shards_of in cuts:
        draws = jnp.exp(jax.random.uniform(jax.random.fold_in(own, axis_at), (shards_of,), jnp.float32, smallest / len(cuts), top_value / len(cuts)))
        loudness = loudness * jnp.repeat(draws, shape[axis_at] // shards_of).reshape([-1 if axis == axis_at else 1 for axis in range(len(shape))])
    return loudness


def scatter_about(stream_key, extent, scale, bound, cuts=(), held_as=jnp.bfloat16):
    level = levels(stream_key, extent, cuts, -0.22, 0.18) if cuts else 1.0
    entries = jax.random.normal(stream_key, extent, jnp.float32) * scale * level
    return jnp.minimum(jnp.maximum(entries, -bound), bound).astype(held_as)


def setup_inputs(seed: int = 0) -> dict:
    streams_of = jax.random.split(jax.random.key(seed), 5)
    return {
        "frames": scatter_about(streams_of[0], (FRAMES, HEIGHT_ROWS, CHANNELS, COLS), 1.0, 6.0, ((0, 2), (1, 4), (2, 4))),
        "grad_out": scatter_about(streams_of[1], (FRAMES, HEIGHT_ROWS, CHANNELS, COLS), 1.0, 6.0, ((0, 2), (1, 4), (2, 4))),
        "weight_one": scatter_about(streams_of[2], (CHANNELS, 3, 3, 3, CHANNELS), (27 * CHANNELS) ** -0.5, 0.078125, ((0, 4),)),
        "weight_two": scatter_about(streams_of[3], (CHANNELS, 3, 3, 3, CHANNELS), (27 * CHANNELS) ** -0.5, 0.078125, ((0, 4),)),
    }


def product(form, left, right):
    return jnp.einsum(form, left.astype(jnp.float32), right.astype(jnp.float32), precision=lax.Precision.HIGHEST)


def forward_taps(padded, weight):
    frame_count = padded.shape[0] - 2
    row_count = padded.shape[1] - 2
    col_count = padded.shape[3] - 2
    summed = jnp.zeros((frame_count, row_count, weight.shape[0], col_count), jnp.float32)
    for time_tap in range(3):
        for row_tap in range(3):
            for col_tap in range(3):
                window = padded[time_tap:time_tap + frame_count, row_tap:row_tap + row_count, :, col_tap:col_tap + col_count]
                summed = summed + product("frcw,oc->frow", window, weight[:, time_tap, row_tap, col_tap, :])
    return summed


def backward_taps(padded, weight):
    frame_count = padded.shape[0] - 2
    row_count = padded.shape[1] - 2
    col_count = padded.shape[3] - 2
    summed = jnp.zeros((frame_count, row_count, weight.shape[4], col_count), jnp.float32)
    for time_tap in range(3):
        for row_tap in range(3):
            for col_tap in range(3):
                window = padded[2 - time_tap:2 - time_tap + frame_count, 2 - row_tap:2 - row_tap + row_count, :, 2 - col_tap:2 - col_tap + col_count]
                summed = summed + product("frow,oc->frcw", window, weight[:, time_tap, row_tap, col_tap, :])
    return summed


def forward_filter(padded, gradient):
    frame_count, row_count, out_width, col_count = gradient.shape
    pieces = []
    for time_tap in range(3):
        for row_tap in range(3):
            for col_tap in range(3):
                window = padded[time_tap:time_tap + frame_count, row_tap:row_tap + row_count, :, col_tap:col_tap + col_count]
                pieces.append(product("frcw,frow->oc", window, gradient))
    return jnp.stack(pieces, 1).reshape(out_width, 3, 3, 3, padded.shape[2])


def backward_filter(source, padded):
    frame_count, row_count, in_width, col_count = source.shape
    pieces = []
    for time_tap in range(3):
        for row_tap in range(3):
            for col_tap in range(3):
                window = padded[2 - time_tap:2 - time_tap + frame_count, 2 - row_tap:2 - row_tap + row_count, :, 2 - col_tap:2 - col_tap + col_count]
                pieces.append(product("frcw,frow->oc", source, window))
    return jnp.stack(pieces, 1).reshape(padded.shape[2], 3, 3, 3, in_width)


def reference(frames, grad_out, weight_one, weight_two):
    frames_padded = jnp.pad(frames, ((2, 0), (1, 1), (0, 0), (1, 1)))
    pre = forward_taps(frames_padded, weight_one)
    act = jax.nn.silu(pre).astype(jnp.bfloat16)
    grads_padded = jnp.pad(grad_out, ((0, 2), (1, 1), (0, 0), (1, 1)))
    grad_act = backward_taps(grads_padded, weight_two)
    sigmoid_pre = jax.nn.sigmoid(pre)
    grad_pre = (grad_act * sigmoid_pre * (1.0 + pre * (1.0 - sigmoid_pre))).astype(jnp.bfloat16)
    pre_padded = jnp.pad(grad_pre, ((0, 2), (1, 1), (0, 0), (1, 1)))
    grad_frames = backward_taps(pre_padded, weight_one).astype(jnp.bfloat16)
    grad_one = forward_filter(frames_padded, grad_pre)
    grad_two = backward_filter(act, grads_padded)
    return (grad_frames, grad_one, grad_two)
```

```python
import functools

import jax
import jax.numpy as jnp
from jax import lax
from jax.experimental import pallas as pl
from jax.experimental.pallas import tpu as pltpu
from jax.sharding import PartitionSpec as P

BF16 = jnp.bfloat16
F32 = jnp.float32
MESH = pl.DeviceIdType.MESH
HALO = 5


def moved_cols(block, offset):
    lane = lax.broadcasted_iota(jnp.int32, block.shape, 1)
    cols = block.shape[1]
    if offset > 0:
        return jnp.where(lane == cols - 1, 0.0, pltpu.roll(block, cols - 1, 1))
    return jnp.where(lane == 0, 0.0, pltpu.roll(block, 1, 1))


def kernel(
    sizes,
    frames, gout, w1, w2,
    gf_out, g1_out, g2_out,
    x, g, gsh, gp, gpsh, w1t, w2t, pre, ga, gain, act, gf, gfin,
    town, tsend, trecv, hown, hsend, hrecv, fin,
    z_send, z_recv, xh_send, xh_recv, gh_send, gh_recv,
    t_send, t_recv, h_send, h_recv, a_send, a_recv, p_send, p_recv,
):
    T, H, Z = sizes
    F, R, C, J = frames.shape
    CC = C * Z
    O = C
    slabs = F * R
    part = 3 * O // H
    tm, h, z = lax.axis_index("tm"), lax.axis_index("height"), lax.axis_index("chan")
    pair = tm + 1 - 2 * lax.rem(tm, 2)
    parity = lax.rem(tm, 2)

    up, down = h > 0, h < H - 1
    has_prev, has_next = tm > 0, tm < T - 1

    def zpeer(d):
        return {"chan": lax.rem(z + d, Z)}

    def hpeer(d):
        return {"height": lax.rem(h + d, H)}

    barrier = pltpu.get_barrier_semaphore()
    for d in range(1, Z):
        pl.semaphore_signal(barrier, inc=1, device_id=zpeer(d), device_id_type=MESH)
    for d in range(1, H):
        pl.semaphore_signal(barrier, inc=1, device_id=hpeer(d), device_id_type=MESH)
    for cond_t, dt in ((has_prev, -1), (has_next, 1)):
        @pl.when(cond_t)
        def _(dt=dt):
            pl.semaphore_signal(barrier, inc=1, device_id={"tm": tm + dt}, device_id_type=MESH)
        for cond_h, dh in ((up, -1), (down, 1)):
            @pl.when(jnp.logical_and(cond_t, cond_h))
            def _(dt=dt, dh=dh):
                pl.semaphore_signal(
                    barrier, inc=1, device_id={"tm": tm + dt, "height": h + dh}, device_id_type=MESH
                )
    n_t = jnp.where(has_prev, 1, 0) + jnp.where(has_next, 1, 0)
    n_h = jnp.where(up, 1, 0) + jnp.where(down, 1, 0)
    pl.semaphore_wait(barrier, (Z - 1) + (H - 1) + n_t + n_t * n_h)

    pending = []

    def remote(src, dst, ssem, rsem, dev):
        return pltpu.make_async_remote_copy(
            src_ref=src, dst_ref=dst, send_sem=ssem, recv_sem=rsem, device_id=dev, device_id_type=MESH
        )

    def send(copy):
        copy.start()
        pending.append((None, copy))
        return copy

    def halo(ext, dt, chan_slice, ssems, rsems):
        o0, f0 = (F, 0) if dt > 0 else (0, F)
        to_t = has_next if dt > 0 else has_prev
        from_t = has_prev if dt > 0 else has_next

        def at(frame, row, rows):
            return ext.at[pl.ds(frame, F), pl.ds(row, rows), chan_slice, :]

        plan = [
            (to_t, from_t, at(o0, 1, R), at(f0, 1, R), {"tm": tm + dt}),
            (down, up, at(o0, R, 1), at(o0, 0, 1), {"height": h + 1}),
            (up, down, at(o0, 1, 1), at(o0, R + 1, 1), {"height": h - 1}),
            (
                jnp.logical_and(to_t, down), jnp.logical_and(from_t, up),
                at(o0, R, 1), at(f0, 0, 1), {"tm": tm + dt, "height": h + 1},
            ),
            (
                jnp.logical_and(to_t, up), jnp.logical_and(from_t, down),
                at(o0, 1, 1), at(f0, R + 1, 1), {"tm": tm + dt, "height": h - 1},
            ),
        ]
        waits = []
        for k, (go, come, src, dst, dev) in enumerate(plan):
            copy = remote(src, dst, ssems[k], rsems[k], dev)
            pl.when(go)(copy.start)
            pending.append((go, copy))
            waits.append((come, copy))
        return waits

    def arrive(waits):
        for come, copy in waits:
            pl.when(come)(copy.wait_recv)

    def zero_edges(ext, dt):
        f0 = 0 if dt > 0 else F
        blank = jnp.logical_not(has_prev if dt > 0 else has_next)

        @pl.when(blank)
        def _():
            ext[f0 : f0 + F] = jnp.zeros((F,) + ext.shape[1:], ext.dtype)

        @pl.when(jnp.logical_not(up))
        def _():
            ext[:, 0] = jnp.zeros((2 * F,) + ext.shape[2:], ext.dtype)

        @pl.when(jnp.logical_not(down))
        def _():
            ext[:, R + 1] = jnp.zeros((2 * F,) + ext.shape[2:], ext.dtype)

    def chunk(index):
        return pl.ds(pl.multiple_of(index * C, C), C)

    mine = chunk(z)

    z_frames = [
        send(remote(
            frames, x.at[pl.ds(F, F), pl.ds(1, R), mine, :],
            z_send.at[0, d - 1], z_recv.at[0, d - 1], zpeer(d),
        ))
        for d in range(1, Z)
    ]
    g[0:F, 1 : R + 1] = gout[...]
    g_waits = halo(
        g, -1, pl.ds(0, C), [gh_send.at[0, k] for k in range(HALO)], [gh_recv.at[0, k] for k in range(HALO)]
    )
    x[F : 2 * F, 1 : R + 1, mine, :] = frames[...]
    x_waits = [halo(
        x, 1, mine, [xh_send.at[0, k] for k in range(HALO)], [xh_recv.at[0, k] for k in range(HALO)]
    )]
    zero_edges(g, -1)
    zero_edges(gp, -1)
    zero_edges(x, 1)

    @pl.loop(0, 9)
    def _(ab):
        w2t[ab] = w2[ab].T
        w1t[ab] = w1[ab].T

    def spread(src, dst, t, i):
        wide = src[t, i].astype(F32)
        dst[t, i, 0:O] = moved_cols(wide, 1).astype(BF16)
        dst[t, i, O : 2 * O] = src[t, i]
        dst[t, i, 2 * O : 3 * O] = moved_cols(wide, -1).astype(BF16)

    def back(source, weight, out):
        @pl.loop(0, slabs // 2)
        def _(s):
            t, i = s // (R // 2), 2 * lax.rem(s, R // 2)
            total = jnp.zeros((CC, 2 * J), F32)
            for a in range(3):
                for b in range(3):
                    window = jnp.concatenate(
                        [source[t + 2 - a, i + 2 - b], source[t + 2 - a, i + 3 - b]], 1
                    )
                    total += jnp.dot(weight[a * 3 + b], window, preferred_element_type=F32)
            out[2 * s] = total[:, :J].astype(BF16)
            out[2 * s + 1] = total[:, J:].astype(BF16)

    def scatter(phase, src, dst):
        return [
            send(remote(
                src.at[:, chunk(lax.rem(z + d, Z)), :], dst.at[d - 1],
                z_send.at[phase, d - 1], z_recv.at[phase, d - 1], zpeer(d),
            ))
            for d in range(1, Z)
        ]

    arrive(g_waits)

    @pl.loop(0, 2 * F * (R + 2))
    def _(s):
        spread(g, gsh, s // (R + 2), lax.rem(s, R + 2))

    back(gsh, w2t, ga)
    z_ga = scatter(1, ga, gain)

    for d in range(1, Z):
        z_frames[d - 1].wait_recv()
        x_waits.append(halo(
            x, 1, chunk(lax.rem(z - d + Z, Z)),
            [xh_send.at[d, k] for k in range(HALO)], [xh_recv.at[d, k] for k in range(HALO)],
        ))
    for waits in x_waits:
        arrive(waits)

    @pl.loop(0, slabs // 2)
    def _(s):
        t, i = s // (R // 2), 2 * lax.rem(s, R // 2)
        total = jnp.zeros((3 * O, 2 * J), F32)
        for a in range(3):
            for b in range(3):
                window = jnp.concatenate([x[t + a, i + b], x[t + a, i + b + 1]], 1)
                total += jnp.dot(w1[a * 3 + b], window, preferred_element_type=F32)
        for half in range(2):
            cols = total[:, half * J : (half + 1) * J]
            value = moved_cols(cols[0:O], -1) + cols[O : 2 * O] + moved_cols(cols[2 * O :], 1)
            pre[2 * s + half] = value
            act[2 * s + half, mine, :] = (value * jax.nn.sigmoid(value)).astype(BF16)

    z_act = [
        send(remote(
            act.at[:, mine, :], act.at[:, mine, :],
            z_send.at[2, d - 1], z_recv.at[2, d - 1], zpeer(d),
        ))
        for d in range(1, Z)
    ]

    for copy in z_ga:
        copy.wait_recv()

    @pl.loop(0, slabs)
    def _(s):
        t, i = s // R, lax.rem(s, R)
        total = ga[s, mine, :].astype(F32)
        for d in range(1, Z):
            total += gain[d - 1, s].astype(F32)
        value = pre[s]
        sig = jax.nn.sigmoid(value)
        gp[t, i + 1] = (total * sig * (1.0 + value * (1.0 - sig))).astype(BF16)

    gp_waits = halo(
        gp, -1, pl.ds(0, C), [gh_send.at[1, k] for k in range(HALO)], [gh_recv.at[1, k] for k in range(HALO)]
    )

    @pl.loop(0, slabs)
    def _(s):
        spread(gp, gpsh, s // R, lax.rem(s, R) + 1)

    def keep(f, ab, value):
        left, right = value[:, :J], value[:, J:]
        town[f, ab] = jnp.where(parity == 0, left, right)
        tsend[f, ab] = jnp.where(parity == 0, right, left).astype(BF16)

    def to_pair(f):
        return send(remote(tsend.at[f], trecv.at[f], t_send.at[f], t_recv.at[f], {"tm": pair}))

    nt = (((1,), (1,)), ((), ()))

    def row_of(source, t0, i0):
        return jnp.concatenate([source[t0 + s // R, i0 + s % R] for s in range(slabs)], 1)

    @pl.loop(0, 9)
    def _(ab):
        left = row_of(gpsh, 0, 1)
        right = row_of(x, ab // 3, lax.rem(ab, 3))
        keep(0, ab, lax.dot_general(left, right, nt, preferred_element_type=F32))

    t_copies = [to_pair(0)]

    arrive(gp_waits)

    @pl.loop(0, F * (R + 2))
    def _(s):
        spread(gp, gpsh, F + s // (R + 2), lax.rem(s, R + 2))

    for t in range(F):
        for i in (0, R + 1):
            spread(gp, gpsh, t, i)
    back(gpsh, w1t, gf)
    z_gf = scatter(3, gf, gfin)

    def from_pair(f):
        t_copies[f].wait_recv()

        @pl.loop(0, 9)
        def _(ab):
            total = town[f, ab] + trecv[f, ab].astype(F32)
            hown[f, ab] = total
            hsend[f, ab] = total.astype(BF16)

        return [
            send(remote(
                hsend.at[f, :, pl.ds(pl.multiple_of(lax.rem(h + d, H) * part, part), part), :],
                hrecv.at[f, d - 1],
                h_send.at[f, d - 1], h_recv.at[f, d - 1], hpeer(d),
            ))
            for d in range(1, H)
        ]

    def from_rows(f, copies):
        for copy in copies:
            copy.wait_recv()
        rows = pl.ds(pl.multiple_of(h * part, part), part)

        @pl.loop(0, 9)
        def _(ab):
            total = hown[f, ab, rows, :]
            for d in range(1, H):
                total += hrecv[f, d - 1, ab].astype(F32)
            fin[f, parity, ab, rows, :] = total.astype(BF16)

        block = fin.at[f, parity, :, rows, :]
        return [
            send(remote(block, block, a_send.at[f, d - 1], a_recv.at[f, d - 1], hpeer(d)))
            for d in range(1, H)
        ]

    def to_other(f, copies):
        for copy in copies:
            copy.wait_recv()
        half = fin.at[f, parity]
        return send(remote(half, half, p_send.at[f], p_recv.at[f], {"tm": pair}))

    h_one = from_pair(0)

    for copy in z_act:
        copy.wait_recv()

    @pl.loop(0, 9)
    def _(ab):
        left = row_of(gsh, 2 - ab // 3, 2 - lax.rem(ab, 3))
        right = jnp.concatenate([act[s] for s in range(slabs)], 1)
        keep(1, ab, lax.dot_general(left, right, nt, preferred_element_type=F32))

    t_copies.append(to_pair(1))
    a_one = from_rows(0, h_one)
    h_two = from_pair(1)
    p_one = to_other(0, a_one)
    a_two = from_rows(1, h_two)

    for copy in z_gf:
        copy.wait_recv()

    @pl.loop(0, slabs)
    def _(s):
        total = gf[s, mine, :].astype(F32)
        for d in range(1, Z):
            total += gfin[d - 1, s].astype(F32)
        gf_out[s // R, lax.rem(s, R)] = total.astype(BF16)

    p_two = to_other(1, a_two)
    p_one.wait_recv()
    g1_out[...] = fin[0]
    p_two.wait_recv()
    g2_out[...] = fin[1]

    for go, copy in pending:
        if go is None:
            copy.wait_send()
        else:
            pl.when(go)(copy.wait_send)


def on_device(sizes, frames, grad_out, weight_one, weight_two):
    T, H, Z = sizes
    F, R, C, J = frames.shape
    CC, slabs, part = C * Z, F * R, 3 * C // H

    def taps_first(weight):
        return weight.transpose(1, 2, 3, 0, 4).reshape(9, 3 * C, CC)

    dma = pltpu.SemaphoreType.DMA
    ext = (2 * F, R + 2)
    scratch = [
        pltpu.VMEM(ext + (CC, J), BF16),
        pltpu.VMEM(ext + (C, J), BF16),
        pltpu.VMEM(ext + (3 * C, J), BF16),
        pltpu.VMEM(ext + (C, J), BF16),
        pltpu.VMEM(ext + (3 * C, J), BF16),
        pltpu.VMEM((9, CC, 3 * C), BF16),
        pltpu.VMEM((9, CC, 3 * C), BF16),
        pltpu.VMEM((slabs, C, J), F32),
        pltpu.VMEM((slabs, CC, J), BF16),
        pltpu.VMEM((Z - 1, slabs, C, J), BF16),
        pltpu.VMEM((slabs, CC, J), BF16),
        pltpu.VMEM((slabs, CC, J), BF16),
        pltpu.VMEM((Z - 1, slabs, C, J), BF16),
        pltpu.VMEM((2, 9, 3 * C, CC // 2), F32),
        pltpu.VMEM((2, 9, 3 * C, CC // 2), BF16),
        pltpu.VMEM((2, 9, 3 * C, CC // 2), BF16),
        pltpu.VMEM((2, 9, 3 * C, CC // 2), F32),
        pltpu.VMEM((2, 9, 3 * C, CC // 2), BF16),
        pltpu.VMEM((2, H - 1, 9, part, CC // 2), BF16),
        pltpu.VMEM((2, 2, 9, 3 * C, CC // 2), BF16),
        dma((4, Z - 1)), dma((4, Z - 1)),
        dma((Z, HALO)), dma((Z, HALO)),
        dma((2, HALO)), dma((2, HALO)),
        dma((2,)), dma((2,)),
        dma((2, H - 1)), dma((2, H - 1)),
        dma((2, H - 1)), dma((2, H - 1)),
        dma((2,)), dma((2,)),
    ]
    vmem = pl.BlockSpec(memory_space=pltpu.VMEM)
    grad_frames, one, two = pl.pallas_call(
        functools.partial(kernel, sizes),
        out_shape=(
            jax.ShapeDtypeStruct((F, R, C, J), BF16),
            jax.ShapeDtypeStruct((2, 9, 3 * C, CC // 2), BF16),
            jax.ShapeDtypeStruct((2, 9, 3 * C, CC // 2), BF16),
        ),
        in_specs=[vmem] * 4,
        out_specs=(vmem,) * 3,
        scratch_shapes=scratch,
        compiler_params=pltpu.CompilerParams(
            collective_id=0, has_side_effects=True, vmem_limit_bytes=56 * 1024 * 1024
        ),
    )(frames, grad_out, taps_first(weight_one), taps_first(weight_two))

    def whole(grad):
        grad = grad.astype(F32)
        if T > 2:
            groups = [list(range(0, T, 2)), list(range(1, T, 2))]
            grad = lax.psum(grad, "tm", axis_index_groups=groups)
        grad = grad.reshape(2, 3, 3, 3, C, CC // 2).transpose(4, 1, 2, 3, 0, 5)
        return grad.reshape(C, 3, 3, 3, CC)

    return grad_frames, whole(one), whole(two)


def solution(mesh):
    sizes = (mesh.shape["tm"], mesh.shape["height"], mesh.shape["chan"])
    cells = P("tm", "height", "chan", None)
    filters = P("chan", None, None, None, None)
    return jax.shard_map(
        functools.partial(on_device, sizes),
        mesh=mesh,
        in_specs=(cells, cells, filters, filters),
        out_specs=(cells, filters, filters),
        check_vma=False,
    )
```

```python
import functools

import jax
import jax.numpy as jnp
from jax import lax
from jax.experimental import pallas as pl
from jax.experimental.pallas import tpu as pltpu
from jax.sharding import PartitionSpec as P

BF16 = jnp.bfloat16
F32 = jnp.float32
MESH = pl.DeviceIdType.MESH
HALO = 5


def moved_cols(block, offset):
    lane = lax.broadcasted_iota(jnp.int32, block.shape, 1)
    cols = block.shape[1]
    if offset > 0:
        return jnp.where(lane == cols - 1, 0.0, pltpu.roll(block, cols - 1, 1))
    return jnp.where(lane == 0, 0.0, pltpu.roll(block, 1, 1))


def kernel(
    sizes,
    frames, gout, w1_in, w2_in,
    gf_out, g1_out, g2_out,
    w1, w2, x, g, gsh, gp, gpsh, w1t, w2t, pre, ga, gain, act, gf, gfin, via,
    town, tsend, trecv, hown, hsend, hrecv, fin,
    z_send, z_recv, zz_send, zz_recv, xh_send, xh_recv, gh_send, gh_recv,
    t_send, t_recv, h_send, h_recv, a_send, a_recv, p_send, p_recv, local,
):
    T, H, Z = sizes
    F, R, C, J = frames.shape
    CC = C * Z
    O = C
    slabs = F * R
    part = 3 * O // H
    FAR = 3 if Z == 4 else Z
    tm, h, z = lax.axis_index("tm"), lax.axis_index("height"), lax.axis_index("chan")
    pair = tm + 1 - 2 * lax.rem(tm, 2)
    parity = lax.rem(tm, 2)

    up, down = h > 0, h < H - 1
    has_prev, has_next = tm > 0, tm < T - 1

    def zpeer(d):
        return {"chan": lax.rem(z + d, Z)}

    def hpeer(d):
        return {"height": lax.rem(h + d, H)}

    both = jnp.logical_and

    loads = [
        pltpu.make_async_copy(w2_in, w2, local.at[0]),
        pltpu.make_async_copy(w1_in, w1, local.at[1]),
    ]
    for copy in loads:
        copy.start()

    barrier = pltpu.get_barrier_semaphore()
    for d in range(1, Z):
        pl.semaphore_signal(barrier, inc=1, device_id=zpeer(d), device_id_type=MESH)
    for d in range(1, H):
        pl.semaphore_signal(barrier, inc=1, device_id=hpeer(d), device_id_type=MESH)
    for cond_t, dt in ((has_prev, -1), (has_next, 1)):
        @pl.when(cond_t)
        def _(dt=dt):
            pl.semaphore_signal(barrier, inc=1, device_id={"tm": tm + dt}, device_id_type=MESH)
        for cond_h, dh in ((up, -1), (down, 1)):
            @pl.when(jnp.logical_and(cond_t, cond_h))
            def _(dt=dt, dh=dh):
                pl.semaphore_signal(
                    barrier, inc=1, device_id={"tm": tm + dt, "height": h + dh}, device_id_type=MESH
                )
    n_t = jnp.where(has_prev, 1, 0) + jnp.where(has_next, 1, 0)
    n_h = jnp.where(up, 1, 0) + jnp.where(down, 1, 0)
    pl.semaphore_wait(barrier, (Z - 1) + (H - 1) + n_t + n_t * n_h)

    pending = []

    def remote(src, dst, ssem, rsem, dev):
        return pltpu.make_async_remote_copy(
            src_ref=src, dst_ref=dst, send_sem=ssem, recv_sem=rsem, device_id=dev, device_id_type=MESH
        )

    def send(copy):
        copy.start()
        pending.append((None, copy))
        return copy

    def send_if(go, copy):
        pl.when(go)(copy.start)
        pending.append((go, copy))

    def halo_plan(ext, dt, chan_slice, ssems, rsems):
        o0, f0 = (F, 0) if dt > 0 else (0, F)
        to_t = has_next if dt > 0 else has_prev
        from_t = has_prev if dt > 0 else has_next

        def at(frame, row, rows):
            return ext.at[pl.ds(frame, F), pl.ds(row, rows), chan_slice, :]

        plan = [
            (to_t, from_t, at(o0, 1, R), at(f0, 1, R), {"tm": tm + dt}),
            (down, up, at(o0, R, 1), at(o0, 0, 1), {"height": h + 1}),
            (up, down, at(o0, 1, 1), at(o0, R + 1, 1), {"height": h - 1}),
            (
                both(to_t, down), both(from_t, up),
                at(o0, R, 1), at(f0, 0, 1), {"tm": tm + dt, "height": h + 1},
            ),
            (
                both(to_t, up), both(from_t, down),
                at(o0, 1, 1), at(f0, R + 1, 1), {"tm": tm + dt, "height": h - 1},
            ),
        ]
        return [
            (go, come, remote(src, dst, ssems.at[k], rsems.at[k], dev))
            for k, (go, come, src, dst, dev) in enumerate(plan)
        ]

    def depart(plan):
        for go, _, copy in plan:
            pl.when(go)(copy.start)

    def arrive(plan):
        for _, come, copy in plan:
            pl.when(come)(copy.wait_recv)

    def zero_edges(ext, dt):
        f0 = 0 if dt > 0 else F

        @pl.when(jnp.logical_not(has_prev if dt > 0 else has_next))
        def _():
            ext[f0 : f0 + F] = jnp.zeros((F,) + ext.shape[1:], ext.dtype)

        @pl.when(jnp.logical_not(up))
        def _():
            ext[:, 0] = jnp.zeros((2 * F,) + ext.shape[2:], ext.dtype)

        @pl.when(jnp.logical_not(down))
        def _():
            ext[:, R + 1] = jnp.zeros((2 * F,) + ext.shape[2:], ext.dtype)

    def chunk(index):
        return pl.ds(pl.multiple_of(index * C, C), C)

    mine = chunk(z)

    def near(p):
        return both(z != p, jnp.abs(z - p) < FAR)

    def gather(phase, block):
        for p in sorted(range(Z), key=lambda p: abs(2 * p - Z + 1)):
            send_if(near(p), remote(
                block(z), block(z), z_send.at[phase, p], z_recv.at[phase, z], {"chan": p}
            ))

    def nearest(k):
        low = z < Z // 2
        side = jnp.where(low, z, Z - 1 - z)
        other = jnp.where(k < side, k, k + 1)
        return jnp.where(low, other, Z - 1 - other)

    def gathered(phase, k, block):
        q = nearest(k)
        remote(
            block(q), block(q), z_send.at[phase, q], z_recv.at[phase, q], zpeer(1)
        ).wait_recv()
        if FAR < Z:
            for go, dz in (
                (both(both(q < z, z < Z - 1), z + 1 - q >= FAR), 1),
                (both(both(q > z, z > 0), q + 1 - z >= FAR), -1),
            ):
                send_if(go, remote(
                    block(q), block(q), zz_send.at[phase, k], z_recv.at[phase, q], {"chan": z + dz}
                ))
        return q

    ends = (0, Z - 1) if FAR < Z else ()

    def takes(p):
        return z == (1 if p == Z - 1 else Z - 2)

    def passed(phase, src, p):
        dz = 1 if p == Z - 1 else -1
        return remote(
            src.at[:, pl.ds(p * C, C), :], via.at[phase // 2],
            zz_send.at[phase, 0], zz_recv.at[phase], {"chan": lax.rem(z + dz + Z, Z)},
        )

    def direct(phase, src, dst, p):
        return remote(
            src.at[:, pl.ds(p * C, C), :], dst.at[z], z_send.at[phase, p], z_recv.at[phase, z], {"chan": p}
        )

    def scatter(phase, src, dst):
        for p in ends:
            send_if(z == Z - 1 - p, passed(phase, src, p))
        for p in range(Z):
            go = both(near(p), jnp.logical_not(takes(p))) if p in ends else near(p)
            pl.when(go)(direct(phase, src, dst, p).start)

    def scatter_rest(phase, src, dst):
        for p in ends:
            @pl.when(takes(p))
            def _(p=p):
                passed(phase, src, p).wait_recv()
                rows = slice(p * C, p * C + C)
                src[:, rows, :] = (
                    src[:, rows, :].astype(F32) + via[phase // 2].astype(F32)
                ).astype(BF16)
                direct(phase, src, dst, p).start()
        for p in range(Z):
            pending.append((near(p), direct(phase, src, dst, p)))

    def scattered(phase, src, dst):
        for q in range(Z):
            pl.when(near(q))(remote(
                src.at[:, pl.ds(0, C), :], dst.at[q], z_send.at[phase, q], z_recv.at[phase, q], zpeer(1)
            ).wait_recv)

    def summed(src, dst, s):
        total = src[s, mine, :].astype(F32)
        for q in range(Z):
            total += dst[q, s].astype(F32)
        return total

    def x_block(q):
        return x.at[pl.ds(F, F), pl.ds(1, R), chunk(q), :]

    def act_block(q):
        return act.at[:, chunk(q), :]

    def x_halo(q):
        return halo_plan(x, 1, chunk(q), xh_send.at[q], xh_recv.at[q])

    x[F : 2 * F, 1 : R + 1, mine, :] = frames[...]
    gather(0, x_block)
    g[0:F, 1 : R + 1] = gout[...]
    g_plan = halo_plan(g, -1, pl.ds(0, C), gh_send.at[0], gh_recv.at[0])
    depart(g_plan)
    depart(x_halo(z))
    zero_edges(g, -1)
    zero_edges(gp, -1)
    zero_edges(x, 1)
    for dst in (gain, gfin):
        for q in range(Z):
            @pl.when(jnp.logical_not(near(q)))
            def _(dst=dst, q=q):
                dst[q] = jnp.zeros(dst.shape[1:], dst.dtype)

    loads[0].wait()

    @pl.loop(0, 9)
    def _(ab):
        w2t[ab] = w2[ab].T

    def spread(src, dst, t, i):
        wide = src[t, i].astype(F32)
        dst[t, i, 0:O] = moved_cols(wide, 1).astype(BF16)
        dst[t, i, O : 2 * O] = src[t, i]
        dst[t, i, 2 * O : 3 * O] = moved_cols(wide, -1).astype(BF16)

    def back(source, weight, out):
        @pl.loop(0, slabs // 2)
        def _(s):
            t, i = s // (R // 2), 2 * lax.rem(s, R // 2)
            total = jnp.zeros((CC, 2 * J), F32)
            for a in range(3):
                for b in range(3):
                    window = jnp.concatenate(
                        [source[t + 2 - a, i + 2 - b], source[t + 2 - a, i + 3 - b]], 1
                    )
                    total += jnp.dot(weight[a * 3 + b], window, preferred_element_type=F32)
            out[2 * s] = total[:, :J].astype(BF16)
            out[2 * s + 1] = total[:, J:].astype(BF16)

    arrive(g_plan)

    @pl.loop(0, 2 * F * (R + 2))
    def _(s):
        spread(g, gsh, s // (R + 2), lax.rem(s, R + 2))

    back(gsh, w2t, ga)
    scatter(1, ga, gain)
    loads[1].wait()

    for k in range(Z - 1):
        depart(x_halo(gathered(0, k, x_block)))
    scatter_rest(1, ga, gain)

    @pl.loop(0, 9)
    def _(ab):
        w1t[ab] = w1[ab].T

    for q in range(Z):
        arrive(x_halo(q))

    @pl.loop(0, slabs // 2)
    def _(s):
        t, i = s // (R // 2), 2 * lax.rem(s, R // 2)
        total = jnp.zeros((3 * O, 2 * J), F32)
        for a in range(3):
            for b in range(3):
                window = jnp.concatenate([x[t + a, i + b], x[t + a, i + b + 1]], 1)
                total += jnp.dot(w1[a * 3 + b], window, preferred_element_type=F32)
        for half in range(2):
            cols = total[:, half * J : (half + 1) * J]
            value = moved_cols(cols[0:O], -1) + cols[O : 2 * O] + moved_cols(cols[2 * O :], 1)
            pre[2 * s + half] = value
            act[2 * s + half, mine, :] = (value * jax.nn.sigmoid(value)).astype(BF16)

    scattered(1, ga, gain)

    @pl.loop(0, slabs)
    def _(s):
        t, i = s // R, lax.rem(s, R)
        total = summed(ga, gain, s)
        value = pre[s]
        sig = jax.nn.sigmoid(value)
        gp[t, i + 1] = (total * sig * (1.0 + value * (1.0 - sig))).astype(BF16)

    gp_plan = halo_plan(gp, -1, pl.ds(0, C), gh_send.at[1], gh_recv.at[1])
    depart(gp_plan)
    gather(2, act_block)

    @pl.loop(0, slabs)
    def _(s):
        spread(gp, gpsh, s // R, lax.rem(s, R) + 1)

    nt = (((1,), (1,)), ((), ()))

    def row_of(source, t0, i0):
        return jnp.concatenate([source[t0 + s // R, i0 + s % R] for s in range(slabs)], 1)

    my_rows = pl.ds(pl.multiple_of(h * part, part), part)

    def taps(a):
        return pl.ds(3 * a, 3)

    def to_pair(f, a, left_of, right_of):
        @pl.loop(0, 3)
        def _(b):
            value = lax.dot_general(left_of(a, b), right_of(a, b), nt, preferred_element_type=F32)
            left, right = value[:, :J], value[:, J:]
            town[f, 3 * a + b] = jnp.where(parity == 0, left, right)
            tsend[f, 3 * a + b] = jnp.where(parity == 0, right, left).astype(BF16)

        return send(remote(
            tsend.at[f, taps(a)], trecv.at[f, taps(a)], t_send.at[f, a], t_recv.at[f, a], {"tm": pair}
        ))

    def to_rows(f, a, copy):
        copy.wait_recv()

        @pl.loop(3 * a, 3 * a + 3)
        def _(ab):
            total = town[f, ab] + trecv[f, ab].astype(F32)
            hown[f, ab] = total
            hsend[f, ab] = total.astype(BF16)

        return [
            send(remote(
                hsend.at[f, taps(a), pl.ds(pl.multiple_of(lax.rem(h + d, H) * part, part), part), :],
                hrecv.at[f, d - 1, taps(a)],
                h_send.at[f, a, d - 1], h_recv.at[f, a, d - 1], hpeer(d),
            ))
            for d in range(1, H)
        ]

    def piece(f, a, row):
        return fin.at[f, parity, taps(a), pl.ds(pl.multiple_of(row * part, part), part), :]

    def relay(f, a, d):
        block = piece(f, a, lax.rem(h - d + H, H))
        return send(remote(block, block, p_send.at[f, a, d], p_recv.at[f, a, d], {"tm": pair}))

    def from_rows(f, a, copies):
        for copy in copies:
            copy.wait_recv()

        @pl.loop(3 * a, 3 * a + 3)
        def _(ab):
            total = hown[f, ab, my_rows, :]
            for d in range(1, H):
                total += hrecv[f, d - 1, ab].astype(F32)
            fin[f, parity, ab, my_rows, :] = total.astype(BF16)

        block = piece(f, a, h)
        copies = [
            send(remote(block, block, a_send.at[f, a, d - 1], a_recv.at[f, a, d - 1], hpeer(d)))
            for d in range(1, H)
        ]
        return copies, [relay(f, a, 0)]

    def to_other(f, a, state):
        copies, relays = state
        for d in range(1, H):
            copies[d - 1].wait_recv()
            relays.append(relay(f, a, d))
        return relays

    def first_left(a, b):
        return row_of(gpsh, 0, 1)

    def first_right(a, b):
        return row_of(x, a, b)

    def second_left(a, b):
        return row_of(gsh, 2 - a, 2 - b)

    def second_right(a, b):
        return jnp.concatenate([act[s] for s in range(slabs)], 1)

    one = [to_pair(0, a, first_left, first_right) for a in range(3)]
    one = [to_rows(0, a, one[a]) for a in range(3)]

    arrive(gp_plan)

    @pl.loop(0, F * (R + 2))
    def _(s):
        spread(gp, gpsh, F + s // (R + 2), lax.rem(s, R + 2))

    for t in range(F):
        for i in (0, R + 1):
            spread(gp, gpsh, t, i)
    back(gpsh, w1t, gf)

    for k in range(Z - 1):
        gathered(2, k, act_block)
    scatter(3, gf, gfin)

    two = [to_pair(1, a, second_left, second_right) for a in range(3)]
    one = [from_rows(0, a, one[a]) for a in range(3)]
    two = [to_rows(1, a, two[a]) for a in range(3)]
    scatter_rest(3, gf, gfin)
    one = [to_other(0, a, one[a]) for a in range(3)]
    two = [from_rows(1, a, two[a]) for a in range(3)]

    for relays in one:
        for copy in relays:
            copy.wait_recv()
    stores = [pltpu.make_async_copy(fin.at[0], g1_out, local.at[2])]
    stores[0].start()
    two = [to_other(1, a, two[a]) for a in range(3)]
    scattered(3, gf, gfin)

    @pl.loop(0, slabs)
    def _(s):
        gf_out[s // R, lax.rem(s, R)] = summed(gf, gfin, s).astype(BF16)

    for relays in two:
        for copy in relays:
            copy.wait_recv()
    stores.append(pltpu.make_async_copy(fin.at[1], g2_out, local.at[3]))
    stores[1].start()

    for go, copy in pending:
        if go is None:
            copy.wait_send()
        else:
            pl.when(go)(copy.wait_send)
    for plan in [g_plan, gp_plan] + [x_halo(q) for q in range(Z)]:
        for go, _, copy in plan:
            pl.when(go)(copy.wait_send)
    for copy in stores:
        copy.wait()


def on_device(sizes, frames, grad_out, weight_one, weight_two):
    T, H, Z = sizes
    F, R, C, J = frames.shape
    CC, slabs, part = C * Z, F * R, 3 * C // H

    def taps_first(weight):
        return weight.transpose(1, 2, 3, 0, 4).reshape(9, 3 * C, CC)

    dma = pltpu.SemaphoreType.DMA
    ext = (2 * F, R + 2)
    scratch = [
        pltpu.VMEM((9, 3 * C, CC), BF16),
        pltpu.VMEM((9, 3 * C, CC), BF16),
        pltpu.VMEM(ext + (CC, J), BF16),
        pltpu.VMEM(ext + (C, J), BF16),
        pltpu.VMEM(ext + (3 * C, J), BF16),
        pltpu.VMEM(ext + (C, J), BF16),
        pltpu.VMEM(ext + (3 * C, J), BF16),
        pltpu.VMEM((9, CC, 3 * C), BF16),
        pltpu.VMEM((9, CC, 3 * C), BF16),
        pltpu.VMEM((slabs, C, J), F32),
        pltpu.VMEM((slabs, CC, J), BF16),
        pltpu.VMEM((Z, slabs, C, J), BF16),
        pltpu.VMEM((slabs, CC, J), BF16),
        pltpu.VMEM((slabs, CC, J), BF16),
        pltpu.VMEM((Z, slabs, C, J), BF16),
        pltpu.VMEM((2, slabs, C, J), BF16),
        pltpu.VMEM((2, 9, 3 * C, CC // 2), F32),
        pltpu.VMEM((2, 9, 3 * C, CC // 2), BF16),
        pltpu.VMEM((2, 9, 3 * C, CC // 2), BF16),
        pltpu.VMEM((2, 9, 3 * C, CC // 2), F32),
        pltpu.VMEM((2, 9, 3 * C, CC // 2), BF16),
        pltpu.VMEM((2, H - 1, 9, part, CC // 2), BF16),
        pltpu.VMEM((2, 2, 9, 3 * C, CC // 2), BF16),
        dma((4, Z)), dma((4, Z)), dma((4, Z)), dma((4,)),
        dma((Z, HALO)), dma((Z, HALO)), dma((2, HALO)), dma((2, HALO)),
        dma((2, 3)), dma((2, 3)), dma((2, 3, H - 1)), dma((2, 3, H - 1)),
        dma((2, 3, H - 1)), dma((2, 3, H - 1)), dma((2, 3, H)), dma((2, 3, H)), dma((4,)),
    ]
    vmem = pl.BlockSpec(memory_space=pltpu.VMEM)
    hbm = pl.BlockSpec(memory_space=pl.ANY)
    grad_frames, one, two = pl.pallas_call(
        functools.partial(kernel, sizes),
        out_shape=(
            jax.ShapeDtypeStruct((F, R, C, J), BF16),
            jax.ShapeDtypeStruct((2, 9, 3 * C, CC // 2), BF16),
            jax.ShapeDtypeStruct((2, 9, 3 * C, CC // 2), BF16),
        ),
        in_specs=[vmem, vmem, hbm, hbm],
        out_specs=(vmem, hbm, hbm),
        scratch_shapes=scratch,
        compiler_params=pltpu.CompilerParams(
            collective_id=0, has_side_effects=True, vmem_limit_bytes=56 * 1024 * 1024
        ),
    )(frames, grad_out, taps_first(weight_one), taps_first(weight_two))

    def whole(grad):
        grad = grad.astype(F32)
        if T > 2:
            groups = [list(range(0, T, 2)), list(range(1, T, 2))]
            grad = lax.psum(grad, "tm", axis_index_groups=groups)
        grad = grad.reshape(2, 3, 3, 3, C, CC // 2).transpose(4, 1, 2, 3, 0, 5)
        return grad.reshape(C, 3, 3, 3, CC)

    return grad_frames, whole(one), whole(two)


def solution(mesh):
    sizes = (mesh.shape["tm"], mesh.shape["height"], mesh.shape["chan"])
    cells = P("tm", "height", "chan", None)
    filters = P("chan", None, None, None, None)
    return jax.shard_map(
        functools.partial(on_device, sizes),
        mesh=mesh,
        in_specs=(cells, cells, filters, filters),
        out_specs=(cells, filters, filters),
        check_vma=False,
    )
```

```python
import functools

import jax
import jax.numpy as jnp
from jax import lax
from jax.experimental import pallas as pl
from jax.experimental.pallas import tpu as pltpu
from jax.sharding import PartitionSpec as P

BF16 = jnp.bfloat16
F32 = jnp.float32
MESH = pl.DeviceIdType.MESH
HALO = 5


def moved_cols(block, offset):
    lane = lax.broadcasted_iota(jnp.int32, block.shape, 1)
    cols = block.shape[1]
    if offset > 0:
        return jnp.where(lane == cols - 1, 0.0, pltpu.roll(block, cols - 1, 1))
    return jnp.where(lane == 0, 0.0, pltpu.roll(block, 1, 1))


def kernel(
    sizes,
    frames, gout, w1_in, w2_in,
    gf_out, g1_out, g2_out,
    w1, w2, x, g, gsh, gp, gpsh, w1t, w2t, pre, ga, gain, act, gf, gfin, via,
    town, tsend, trecv, hown, hsend, hrecv, fin,
    z_send, z_recv, zz_send, zz_recv, xh_send, xh_recv, gh_send, gh_recv,
    t_send, t_recv, h_send, h_recv, a_send, a_recv, p_send, p_recv, local,
):
    T, H, Z = sizes
    F, R, C, J = gf_out.shape
    CC = C * Z
    O = C
    slabs = F * R
    part = 3 * O // H
    FAR = 3 if Z == 4 else Z
    tm, h, z = lax.axis_index("tm"), lax.axis_index("height"), lax.axis_index("chan")
    pair = tm + 1 - 2 * lax.rem(tm, 2)
    parity = lax.rem(tm, 2)

    up, down = h > 0, h < H - 1
    has_prev, has_next = tm > 0, tm < T - 1

    def zpeer(d):
        return {"chan": lax.rem(z + d, Z)}

    def hpeer(d):
        return {"height": lax.rem(h + d, H)}

    both = jnp.logical_and

    loads = [
        pltpu.make_async_copy(w2_in, w2, local.at[0]),
        pltpu.make_async_copy(w1_in, w1, local.at[1]),
        pltpu.make_async_copy(
            frames,
            x.at[pl.ds(F, F), pl.ds(1, R), pl.ds(pl.multiple_of(z * C, C), C), :],
            local.at[4],
        ),
        pltpu.make_async_copy(gout, g.at[pl.ds(0, F), pl.ds(1, R)], local.at[5]),
    ]
    for k in (2, 3, 0, 1):
        loads[k].start()

    barrier = pltpu.get_barrier_semaphore()
    for d in range(1, Z):
        pl.semaphore_signal(barrier, inc=1, device_id=zpeer(d), device_id_type=MESH)
    for d in range(1, H):
        pl.semaphore_signal(barrier, inc=1, device_id=hpeer(d), device_id_type=MESH)
    for cond_t, dt in ((has_prev, -1), (has_next, 1)):
        @pl.when(cond_t)
        def _(dt=dt):
            pl.semaphore_signal(barrier, inc=1, device_id={"tm": tm + dt}, device_id_type=MESH)
        for cond_h, dh in ((up, -1), (down, 1)):
            @pl.when(jnp.logical_and(cond_t, cond_h))
            def _(dt=dt, dh=dh):
                pl.semaphore_signal(
                    barrier, inc=1, device_id={"tm": tm + dt, "height": h + dh}, device_id_type=MESH
                )
    def near(p):
        return both(z != p, jnp.abs(z - p) < FAR)

    def zero_edges(ext, dt):
        f0 = 0 if dt > 0 else F

        @pl.when(jnp.logical_not(has_prev if dt > 0 else has_next))
        def _():
            ext[f0 : f0 + F] = jnp.zeros((F,) + ext.shape[1:], ext.dtype)

        @pl.when(jnp.logical_not(up))
        def _():
            ext[:, 0] = jnp.zeros((2 * F,) + ext.shape[2:], ext.dtype)

        @pl.when(jnp.logical_not(down))
        def _():
            ext[:, R + 1] = jnp.zeros((2 * F,) + ext.shape[2:], ext.dtype)

    zero_edges(g, -1)
    zero_edges(gp, -1)
    zero_edges(x, 1)
    for dst in (gain, gfin):
        for q in range(Z):
            @pl.when(jnp.logical_not(near(q)))
            def _(dst=dst, q=q):
                dst[q] = jnp.zeros(dst.shape[1:], dst.dtype)

    n_t = jnp.where(has_prev, 1, 0) + jnp.where(has_next, 1, 0)
    n_h = jnp.where(up, 1, 0) + jnp.where(down, 1, 0)
    pl.semaphore_wait(barrier, (Z - 1) + (H - 1) + n_t + n_t * n_h)

    pending = []

    def remote(src, dst, ssem, rsem, dev):
        return pltpu.make_async_remote_copy(
            src_ref=src, dst_ref=dst, send_sem=ssem, recv_sem=rsem, device_id=dev, device_id_type=MESH
        )

    def send(copy):
        copy.start()
        pending.append((None, copy))
        return copy

    def send_if(go, copy):
        pl.when(go)(copy.start)
        pending.append((go, copy))

    def halo_plan(ext, dt, chan_slice, ssems, rsems):
        o0, f0 = (F, 0) if dt > 0 else (0, F)
        to_t = has_next if dt > 0 else has_prev
        from_t = has_prev if dt > 0 else has_next

        def at(frame, row, rows):
            return ext.at[pl.ds(frame, F), pl.ds(row, rows), chan_slice, :]

        plan = [
            (to_t, from_t, at(o0, 1, R), at(f0, 1, R), {"tm": tm + dt}),
            (down, up, at(o0, R, 1), at(o0, 0, 1), {"height": h + 1}),
            (up, down, at(o0, 1, 1), at(o0, R + 1, 1), {"height": h - 1}),
            (
                both(to_t, down), both(from_t, up),
                at(o0, R, 1), at(f0, 0, 1), {"tm": tm + dt, "height": h + 1},
            ),
            (
                both(to_t, up), both(from_t, down),
                at(o0, 1, 1), at(f0, R + 1, 1), {"tm": tm + dt, "height": h - 1},
            ),
        ]
        return [
            (go, come, remote(src, dst, ssems.at[k], rsems.at[k], dev))
            for k, (go, come, src, dst, dev) in enumerate(plan)
        ]

    def depart(plan):
        for go, _, copy in plan:
            pl.when(go)(copy.start)

    def arrive(plan):
        for _, come, copy in plan:
            pl.when(come)(copy.wait_recv)

    def chunk(index):
        return pl.ds(pl.multiple_of(index * C, C), C)

    mine = chunk(z)

    def gather(phase, block):
        for p in sorted(range(Z), key=lambda p: abs(2 * p - Z + 1)):
            send_if(near(p), remote(
                block(z), block(z), z_send.at[phase, p], z_recv.at[phase, z], {"chan": p}
            ))

    def nearest(k):
        low = z < Z // 2
        side = jnp.where(low, z, Z - 1 - z)
        other = jnp.where(k < side, k, k + 1)
        return jnp.where(low, other, Z - 1 - other)

    def gathered(phase, k, block):
        q = nearest(k)
        remote(
            block(q), block(q), z_send.at[phase, q], z_recv.at[phase, q], zpeer(1)
        ).wait_recv()
        if FAR < Z:
            for go, dz in (
                (both(both(q < z, z < Z - 1), z + 1 - q >= FAR), 1),
                (both(both(q > z, z > 0), q + 1 - z >= FAR), -1),
            ):
                send_if(go, remote(
                    block(q), block(q), zz_send.at[phase, k], z_recv.at[phase, q], {"chan": z + dz}
                ))
        return q

    ends = (0, Z - 1) if FAR < Z else ()

    def takes(p):
        return z == (1 if p == Z - 1 else Z - 2)

    def passed(phase, src, p):
        dz = 1 if p == Z - 1 else -1
        return remote(
            src.at[:, pl.ds(p * C, C), :], via.at[phase // 2],
            zz_send.at[phase, 0], zz_recv.at[phase], {"chan": lax.rem(z + dz + Z, Z)},
        )

    def direct(phase, src, dst, p):
        return remote(
            src.at[:, pl.ds(p * C, C), :], dst.at[z], z_send.at[phase, p], z_recv.at[phase, z], {"chan": p}
        )

    def scatter(phase, src, dst):
        for p in ends:
            send_if(z == Z - 1 - p, passed(phase, src, p))
        for p in range(Z):
            go = both(near(p), jnp.logical_not(takes(p))) if p in ends else near(p)
            pl.when(go)(direct(phase, src, dst, p).start)

    def scatter_rest(phase, src, dst):
        for p in ends:
            @pl.when(takes(p))
            def _(p=p):
                passed(phase, src, p).wait_recv()
                rows = slice(p * C, p * C + C)
                src[:, rows, :] = (
                    src[:, rows, :].astype(F32) + via[phase // 2].astype(F32)
                ).astype(BF16)
                direct(phase, src, dst, p).start()
        for p in range(Z):
            pending.append((near(p), direct(phase, src, dst, p)))

    def scattered(phase, src, dst):
        for q in range(Z):
            pl.when(near(q))(remote(
                src.at[:, pl.ds(0, C), :], dst.at[q], z_send.at[phase, q], z_recv.at[phase, q], zpeer(1)
            ).wait_recv)

    def summed(src, dst, s):
        total = src[s, mine, :].astype(F32)
        for q in range(Z):
            total += dst[q, s].astype(F32)
        return total

    def x_block(q):
        return x.at[pl.ds(F, F), pl.ds(1, R), chunk(q), :]

    def act_block(q):
        return act.at[:, chunk(q), :]

    def x_halo(q):
        return halo_plan(x, 1, chunk(q), xh_send.at[q], xh_recv.at[q])

    loads[2].wait()
    gather(0, x_block)
    loads[3].wait()
    g_plan = halo_plan(g, -1, pl.ds(0, C), gh_send.at[0], gh_recv.at[0])
    depart(g_plan)
    depart(x_halo(z))
    def turned(weight, out):
        flat = weight[...].reshape(27 * O, CC)
        for k in range(0, 27 * O, 2 * J):
            end = min(k + 2 * J, 27 * O)
            out[:, k:end] = flat[k:end].T

    loads[0].wait()

    turned(w2, w2t)

    def spread(src, dst, t, i):
        wide = src[t, i].astype(F32)
        dst[t, i, 0:O] = moved_cols(wide, 1).astype(BF16)
        dst[t, i, O : 2 * O] = src[t, i]
        dst[t, i, 2 * O : 3 * O] = moved_cols(wide, -1).astype(BF16)

    def back(source, weight, out):
        @pl.loop(0, slabs // 2)
        def _(s):
            t, i = s // (R // 2), 2 * lax.rem(s, R // 2)
            windows = [
                jnp.concatenate([source[t + 2 - a, i + 2 - b], source[t + 2 - a, i + 3 - b]], 1)
                for a in range(3)
                for b in range(3)
            ]
            total = jnp.dot(weight[...], jnp.concatenate(windows, 0), preferred_element_type=F32)
            out[2 * s] = total[:, :J].astype(BF16)
            out[2 * s + 1] = total[:, J:].astype(BF16)

    arrive(g_plan)

    @pl.loop(0, 2 * F * (R + 2), unroll=4)
    def _(s):
        spread(g, gsh, s // (R + 2), lax.rem(s, R + 2))

    back(gsh, w2t, ga)
    scatter(1, ga, gain)
    loads[1].wait()

    for k in range(Z - 1):
        depart(x_halo(gathered(0, k, x_block)))
    scatter_rest(1, ga, gain)

    turned(w1, w1t)

    for q in range(Z):
        arrive(x_halo(q))

    @pl.loop(0, slabs // 2)
    def _(s):
        t, i = s // (R // 2), 2 * lax.rem(s, R // 2)
        windows = [
            jnp.concatenate([x[t + a, i + b], x[t + a, i + b + 1]], 1)
            for a in range(3)
            for b in range(3)
        ]
        taps_of = jnp.concatenate([w1[ab] for ab in range(9)], 1)
        total = jnp.dot(taps_of, jnp.concatenate(windows, 0), preferred_element_type=F32)
        for half in range(2):
            cols = total[:, half * J : (half + 1) * J]
            value = moved_cols(cols[0:O], -1) + cols[O : 2 * O] + moved_cols(cols[2 * O :], 1)
            pre[2 * s + half] = value
            act[2 * s + half, mine, :] = (value * jax.nn.sigmoid(value)).astype(BF16)

    scattered(1, ga, gain)
    gather(2, act_block)

    @pl.loop(0, slabs, unroll=4)
    def _(s):
        t, i = s // R, lax.rem(s, R)
        total = summed(ga, gain, s)
        value = pre[s]
        sig = jax.nn.sigmoid(value)
        gp[t, i + 1] = (total * sig * (1.0 + value * (1.0 - sig))).astype(BF16)

    gp_plan = halo_plan(gp, -1, pl.ds(0, C), gh_send.at[1], gh_recv.at[1])
    depart(gp_plan)

    @pl.loop(0, slabs, unroll=4)
    def _(s):
        spread(gp, gpsh, s // R, lax.rem(s, R) + 1)

    nt = (((1,), (1,)), ((), ()))

    def row_of(source, t0, i0):
        return jnp.concatenate([source[t0 + s // R, i0 + s % R] for s in range(slabs)], 1)

    my_rows = pl.ds(pl.multiple_of(h * part, part), part)

    def taps(a):
        return pl.ds(3 * a, 3)

    def to_pair(f, a, left_of, right_of):
        @pl.loop(0, 3)
        def _(b):
            value = lax.dot_general(left_of(a, b), right_of(a, b), nt, preferred_element_type=F32)
            left, right = value[:, :J], value[:, J:]
            town[f, 3 * a + b] = jnp.where(parity == 0, left, right)
            tsend[f, 3 * a + b] = jnp.where(parity == 0, right, left).astype(BF16)

        return send(remote(
            tsend.at[f, taps(a)], trecv.at[f, taps(a)], t_send.at[f, a], t_recv.at[f, a], {"tm": pair}
        ))

    def to_rows(f, a, copy):
        copy.wait_recv()

        @pl.loop(3 * a, 3 * a + 3, unroll=3)
        def _(ab):
            total = town[f, ab] + trecv[f, ab].astype(F32)
            hown[f, ab] = total
            hsend[f, ab] = total.astype(BF16)

        return [
            send(remote(
                hsend.at[f, taps(a), pl.ds(pl.multiple_of(lax.rem(h + d, H) * part, part), part), :],
                hrecv.at[f, d - 1, taps(a)],
                h_send.at[f, a, d - 1], h_recv.at[f, a, d - 1], hpeer(d),
            ))
            for d in range(1, H)
        ]

    def piece(f, a, row):
        return fin.at[f, parity, taps(a), pl.ds(pl.multiple_of(row * part, part), part), :]

    def relay(f, a, d):
        block = piece(f, a, lax.rem(h - d + H, H))
        return send(remote(block, block, p_send.at[f, a, d], p_recv.at[f, a, d], {"tm": pair}))

    def from_rows(f, a, copies):
        for copy in copies:
            copy.wait_recv()

        @pl.loop(3 * a, 3 * a + 3, unroll=3)
        def _(ab):
            total = hown[f, ab, my_rows, :]
            for d in range(1, H):
                total += hrecv[f, d - 1, ab].astype(F32)
            fin[f, parity, ab, my_rows, :] = total.astype(BF16)

        block = piece(f, a, h)
        copies = [
            send(remote(block, block, a_send.at[f, a, d - 1], a_recv.at[f, a, d - 1], hpeer(d)))
            for d in range(1, H)
        ]
        return copies, [relay(f, a, 0)]

    def to_other(f, a, state):
        copies, relays = state
        for d in range(1, H):
            copies[d - 1].wait_recv()
            relays.append(relay(f, a, d))
        return relays

    def first_left(a, b):
        return row_of(gpsh, 0, 1)

    def first_right(a, b):
        return row_of(x, a, b)

    def second_left(a, b):
        return row_of(gsh, 2 - a, 2 - b)

    def second_right(a, b):
        return jnp.concatenate([act[s] for s in range(slabs)], 1)

    one = [to_pair(0, a, first_left, first_right) for a in range(3)]
    one = [to_rows(0, a, one[a]) for a in range(3)]

    arrive(gp_plan)

    @pl.loop(0, F * (R + 2), unroll=4)
    def _(s):
        spread(gp, gpsh, F + s // (R + 2), lax.rem(s, R + 2))

    for t in range(F):
        for i in (0, R + 1):
            spread(gp, gpsh, t, i)
    back(gpsh, w1t, gf)

    for k in range(Z - 1):
        gathered(2, k, act_block)
    scatter(3, gf, gfin)

    two = [to_pair(1, a, second_left, second_right) for a in range(3)]
    one = [from_rows(0, a, one[a]) for a in range(3)]
    two = [to_rows(1, a, two[a]) for a in range(3)]
    scatter_rest(3, gf, gfin)
    one = [to_other(0, a, one[a]) for a in range(3)]
    two = [from_rows(1, a, two[a]) for a in range(3)]

    for relays in one:
        for copy in relays:
            copy.wait_recv()
    stores = [pltpu.make_async_copy(fin.at[0], g1_out, local.at[2])]
    stores[0].start()
    two = [to_other(1, a, two[a]) for a in range(3)]
    scattered(3, gf, gfin)

    @pl.loop(0, slabs, unroll=4)
    def _(s):
        gf_out[s // R, lax.rem(s, R)] = summed(gf, gfin, s).astype(BF16)

    for relays in two:
        for copy in relays:
            copy.wait_recv()
    stores.append(pltpu.make_async_copy(fin.at[1], g2_out, local.at[3]))
    stores[1].start()

    for go, copy in pending:
        if go is None:
            copy.wait_send()
        else:
            pl.when(go)(copy.wait_send)
    for plan in [g_plan, gp_plan] + [x_halo(q) for q in range(Z)]:
        for go, _, copy in plan:
            pl.when(go)(copy.wait_send)
    for copy in stores:
        copy.wait()


def on_device(sizes, frames, grad_out, weight_one, weight_two):
    T, H, Z = sizes
    F, R, C, J = frames.shape
    CC, slabs, part = C * Z, F * R, 3 * C // H

    def taps_first(weight):
        return weight.transpose(1, 2, 3, 0, 4).reshape(9, 3 * C, CC)

    dma = pltpu.SemaphoreType.DMA
    ext = (2 * F, R + 2)
    scratch = [
        pltpu.VMEM((9, 3 * C, CC), BF16),
        pltpu.VMEM((9, 3 * C, CC), BF16),
        pltpu.VMEM(ext + (CC, J), BF16),
        pltpu.VMEM(ext + (C, J), BF16),
        pltpu.VMEM(ext + (3 * C, J), BF16),
        pltpu.VMEM(ext + (C, J), BF16),
        pltpu.VMEM(ext + (3 * C, J), BF16),
        pltpu.VMEM((CC, 27 * C), BF16),
        pltpu.VMEM((CC, 27 * C), BF16),
        pltpu.VMEM((slabs, C, J), F32),
        pltpu.VMEM((slabs, CC, J), BF16),
        pltpu.VMEM((Z, slabs, C, J), BF16),
        pltpu.VMEM((slabs, CC, J), BF16),
        pltpu.VMEM((slabs, CC, J), BF16),
        pltpu.VMEM((Z, slabs, C, J), BF16),
        pltpu.VMEM((2, slabs, C, J), BF16),
        pltpu.VMEM((2, 9, 3 * C, CC // 2), F32),
        pltpu.VMEM((2, 9, 3 * C, CC // 2), BF16),
        pltpu.VMEM((2, 9, 3 * C, CC // 2), BF16),
        pltpu.VMEM((2, 9, 3 * C, CC // 2), F32),
        pltpu.VMEM((2, 9, 3 * C, CC // 2), BF16),
        pltpu.VMEM((2, H - 1, 9, part, CC // 2), BF16),
        pltpu.VMEM((2, 2, 9, 3 * C, CC // 2), BF16),
        dma((4, Z)), dma((4, Z)), dma((4, Z)), dma((4,)),
        dma((Z, HALO)), dma((Z, HALO)), dma((2, HALO)), dma((2, HALO)),
        dma((2, 3)), dma((2, 3)), dma((2, 3, H - 1)), dma((2, 3, H - 1)),
        dma((2, 3, H - 1)), dma((2, 3, H - 1)), dma((2, 3, H)), dma((2, 3, H)), dma((6,)),
    ]
    vmem = pl.BlockSpec(memory_space=pltpu.VMEM)
    hbm = pl.BlockSpec(memory_space=pl.ANY)
    grad_frames, one, two = pl.pallas_call(
        functools.partial(kernel, sizes),
        out_shape=(
            jax.ShapeDtypeStruct((F, R, C, J), BF16),
            jax.ShapeDtypeStruct((2, 9, 3 * C, CC // 2), BF16),
            jax.ShapeDtypeStruct((2, 9, 3 * C, CC // 2), BF16),
        ),
        in_specs=[hbm] * 4,
        out_specs=(vmem, hbm, hbm),
        scratch_shapes=scratch,
        compiler_params=pltpu.CompilerParams(
            collective_id=0, has_side_effects=True, vmem_limit_bytes=56 * 1024 * 1024
        ),
    )(frames, grad_out, taps_first(weight_one), taps_first(weight_two))

    def widened(cells_in, one_in, two_in, cells_out, one_out, two_out):
        cells_out[...] = cells_in[...]
        for narrow, wide in ((one_in, one_out), (two_in, two_out)):
            for half in range(2):
                wide[:, :, half * CC // 2 : (half + 1) * CC // 2] = narrow[half].astype(F32)

    cells = pl.BlockSpec((F, R, C, J), lambda a: (0, 0, 0, 0))
    narrow = pl.BlockSpec((2, 3, 3 * C, CC // 2), lambda a: (0, a, 0, 0))
    wide = pl.BlockSpec((3, 3 * C, CC), lambda a: (a, 0, 0))
    filters = jax.ShapeDtypeStruct((9, 3 * C, CC), F32)
    grad_frames, one, two = pl.pallas_call(
        widened,
        grid=(3,),
        out_shape=(jax.ShapeDtypeStruct((F, R, C, J), BF16), filters, filters),
        in_specs=[cells, narrow, narrow],
        out_specs=(cells, wide, wide),
        compiler_params=pltpu.CompilerParams(vmem_limit_bytes=56 * 1024 * 1024),
    )(grad_frames, one, two)

    def whole(grad):
        if T > 2:
            groups = [list(range(0, T, 2)), list(range(1, T, 2))]
            grad = lax.psum(grad, "tm", axis_index_groups=groups)
        return grad.reshape(3, 3, 3, C, CC).transpose(3, 0, 1, 2, 4)

    return grad_frames, whole(one), whole(two)


def solution(mesh):
    sizes = (mesh.shape["tm"], mesh.shape["height"], mesh.shape["chan"])
    cells = P("tm", "height", "chan", None)
    filters = P("chan", None, None, None, None)
    return jax.shard_map(
        functools.partial(on_device, sizes),
        mesh=mesh,
        in_specs=(cells, cells, filters, filters),
        out_specs=(cells, filters, filters),
        check_vma=False,
    )
```

```python
import functools

import jax
import jax.numpy as jnp
from jax import lax
from jax.experimental import pallas as pl
from jax.experimental.pallas import tpu as pltpu
from jax.sharding import PartitionSpec as P

BF16 = jnp.bfloat16
F32 = jnp.float32
MESH = pl.DeviceIdType.MESH
HALO = 5


def moved_cols(block, offset):
    lane = lax.broadcasted_iota(jnp.int32, block.shape, 1)
    cols = block.shape[1]
    if offset > 0:
        return jnp.where(lane == cols - 1, 0.0, pltpu.roll(block, cols - 1, 1))
    return jnp.where(lane == 0, 0.0, pltpu.roll(block, 1, 1))


def kernel(
    sizes,
    frames, gout, w1_in, w2_in,
    gf_out, g1_out, g2_out,
    w1, w2, w1c, raw, x, g, gsh, gp, gpsh, w1t, w2t, pre, ga, gain, act, gf, gfin, via,
    town, tsend, trecv, hown, hsend, hrecv, fin,
    z_send, z_recv, zz_send, zz_recv, xh_send, xh_recv, gh_send, gh_recv,
    t_send, t_recv, h_send, h_recv, a_send, a_recv, p_send, p_recv, local,
):
    T, H, Z = sizes
    F, R, C, J = gf_out.shape
    CC = C * Z
    O = C
    slabs = F * R
    part = 3 * O // H
    FAR = 3 if Z == 4 else Z
    tm, h, z = lax.axis_index("tm"), lax.axis_index("height"), lax.axis_index("chan")
    pair = tm + 1 - 2 * lax.rem(tm, 2)
    parity = lax.rem(tm, 2)

    up, down = h > 0, h < H - 1
    has_prev, has_next = tm > 0, tm < T - 1

    def zpeer(d):
        return {"chan": lax.rem(z + d, Z)}

    def hpeer(d):
        return {"height": lax.rem(h + d, H)}

    both = jnp.logical_and

    loads = [
        pltpu.make_async_copy(w2_in, w2, local.at[0]),
        pltpu.make_async_copy(w1_in, w1, local.at[1]),
        pltpu.make_async_copy(
            frames,
            x.at[pl.ds(F, F), pl.ds(1, R), pl.ds(pl.multiple_of(z * C, C), C), :],
            local.at[4],
        ),
        pltpu.make_async_copy(gout, g.at[pl.ds(0, F), pl.ds(1, R)], local.at[5]),
    ]
    for k in (2, 3, 0, 1):
        loads[k].start()

    barrier = pltpu.get_barrier_semaphore()
    for d in range(1, Z):
        pl.semaphore_signal(barrier, inc=1, device_id=zpeer(d), device_id_type=MESH)
    for d in range(1, H):
        pl.semaphore_signal(barrier, inc=1, device_id=hpeer(d), device_id_type=MESH)
    for cond_t, dt in ((has_prev, -1), (has_next, 1)):
        @pl.when(cond_t)
        def _(dt=dt):
            pl.semaphore_signal(barrier, inc=1, device_id={"tm": tm + dt}, device_id_type=MESH)
        for cond_h, dh in ((up, -1), (down, 1)):
            @pl.when(jnp.logical_and(cond_t, cond_h))
            def _(dt=dt, dh=dh):
                pl.semaphore_signal(
                    barrier, inc=1, device_id={"tm": tm + dt, "height": h + dh}, device_id_type=MESH
                )
    def near(p):
        return both(z != p, jnp.abs(z - p) < FAR)

    def zero_edges(ext, dt):
        f0 = 0 if dt > 0 else F

        @pl.when(jnp.logical_not(has_prev if dt > 0 else has_next))
        def _():
            ext[f0 : f0 + F] = jnp.zeros((F,) + ext.shape[1:], ext.dtype)

        @pl.when(jnp.logical_not(up))
        def _():
            ext[:, 0] = jnp.zeros((2 * F,) + ext.shape[2:], ext.dtype)

        @pl.when(jnp.logical_not(down))
        def _():
            ext[:, R + 1] = jnp.zeros((2 * F,) + ext.shape[2:], ext.dtype)

    zero_edges(g, -1)
    zero_edges(gp, -1)
    zero_edges(x, 1)
    for dst in (gain, gfin):
        for q in range(Z):
            @pl.when(jnp.logical_not(near(q)))
            def _(dst=dst, q=q):
                dst[q] = jnp.zeros(dst.shape[1:], dst.dtype)

    n_t = jnp.where(has_prev, 1, 0) + jnp.where(has_next, 1, 0)
    n_h = jnp.where(up, 1, 0) + jnp.where(down, 1, 0)
    pl.semaphore_wait(barrier, (Z - 1) + (H - 1) + n_t + n_t * n_h)

    pending = []

    def remote(src, dst, ssem, rsem, dev):
        return pltpu.make_async_remote_copy(
            src_ref=src, dst_ref=dst, send_sem=ssem, recv_sem=rsem, device_id=dev, device_id_type=MESH
        )

    def send(copy):
        copy.start()
        pending.append((None, copy))
        return copy

    def send_if(go, copy):
        pl.when(go)(copy.start)
        pending.append((go, copy))

    def halo_plan(ext, dt, chan_slice, ssems, rsems):
        o0, f0 = (F, 0) if dt > 0 else (0, F)
        to_t = has_next if dt > 0 else has_prev
        from_t = has_prev if dt > 0 else has_next

        def at(frame, row, rows):
            return ext.at[pl.ds(frame, F), pl.ds(row, rows), chan_slice, :]

        plan = [
            (to_t, from_t, at(o0, 1, R), at(f0, 1, R), {"tm": tm + dt}),
            (down, up, at(o0, R, 1), at(o0, 0, 1), {"height": h + 1}),
            (up, down, at(o0, 1, 1), at(o0, R + 1, 1), {"height": h - 1}),
            (
                both(to_t, down), both(from_t, up),
                at(o0, R, 1), at(f0, 0, 1), {"tm": tm + dt, "height": h + 1},
            ),
            (
                both(to_t, up), both(from_t, down),
                at(o0, 1, 1), at(f0, R + 1, 1), {"tm": tm + dt, "height": h - 1},
            ),
        ]
        return [
            (go, come, remote(src, dst, ssems.at[k], rsems.at[k], dev))
            for k, (go, come, src, dst, dev) in enumerate(plan)
        ]

    def depart(plan):
        for go, _, copy in plan:
            pl.when(go)(copy.start)

    def arrive(plan):
        for _, come, copy in plan:
            pl.when(come)(copy.wait_recv)

    def chunk(index):
        return pl.ds(pl.multiple_of(index * C, C), C)

    mine = chunk(z)

    def gather(phase, block):
        for p in sorted(range(Z), key=lambda p: abs(2 * p - Z + 1)):
            send_if(near(p), remote(
                block(z), block(z), z_send.at[phase, p], z_recv.at[phase, z], {"chan": p}
            ))

    def nearest(k):
        low = z < Z // 2
        side = jnp.where(low, z, Z - 1 - z)
        other = jnp.where(k < side, k, k + 1)
        return jnp.where(low, other, Z - 1 - other)

    def gathered(phase, k, block):
        q = nearest(k)
        remote(
            block(q), block(q), z_send.at[phase, q], z_recv.at[phase, q], zpeer(1)
        ).wait_recv()
        if FAR < Z:
            for go, dz in (
                (both(both(q < z, z < Z - 1), z + 1 - q >= FAR), 1),
                (both(both(q > z, z > 0), q + 1 - z >= FAR), -1),
            ):
                send_if(go, remote(
                    block(q), block(q), zz_send.at[phase, k], z_recv.at[phase, q], {"chan": z + dz}
                ))
        return q

    ends = (0, Z - 1) if FAR < Z else ()

    def takes(p):
        return z == (1 if p == Z - 1 else Z - 2)

    def passed(phase, src, p):
        dz = 1 if p == Z - 1 else -1
        return remote(
            src.at[:, pl.ds(p * C, C), :], via.at[phase // 2],
            zz_send.at[phase, 0], zz_recv.at[phase], {"chan": lax.rem(z + dz + Z, Z)},
        )

    def direct(phase, src, dst, p):
        return remote(
            src.at[:, pl.ds(p * C, C), :], dst.at[z], z_send.at[phase, p], z_recv.at[phase, z], {"chan": p}
        )

    def scatter(phase, src, dst):
        for p in ends:
            send_if(z == Z - 1 - p, passed(phase, src, p))
        for p in range(Z):
            go = both(near(p), jnp.logical_not(takes(p))) if p in ends else near(p)
            pl.when(go)(direct(phase, src, dst, p).start)

    def scatter_rest(phase, src, dst):
        for p in ends:
            @pl.when(takes(p))
            def _(p=p):
                passed(phase, src, p).wait_recv()
                rows = slice(p * C, p * C + C)
                src[:, rows, :] = (
                    src[:, rows, :].astype(F32) + via[phase // 2].astype(F32)
                ).astype(BF16)
                direct(phase, src, dst, p).start()
        for p in range(Z):
            pending.append((near(p), direct(phase, src, dst, p)))

    def scattered(phase, src, dst):
        for q in range(Z):
            pl.when(near(q))(remote(
                src.at[:, pl.ds(0, C), :], dst.at[q], z_send.at[phase, q], z_recv.at[phase, q], zpeer(1)
            ).wait_recv)

    def summed(src, dst, s):
        total = src[s, mine, :].astype(F32)
        for q in range(Z):
            total += dst[q, s].astype(F32)
        return total

    def x_block(q):
        return x.at[pl.ds(F, F), pl.ds(1, R), chunk(q), :]

    def act_block(q):
        return act.at[:, chunk(q), :]

    def x_halo(q):
        return halo_plan(x, 1, chunk(q), xh_send.at[q], xh_recv.at[q])

    loads[2].wait()
    gather(0, x_block)
    loads[3].wait()
    g_plan = halo_plan(g, -1, pl.ds(0, C), gh_send.at[0], gh_recv.at[0])
    depart(g_plan)
    depart(x_halo(z))
    def turned(weight, out):
        flat = weight[...].reshape(27 * O, CC)
        for k in range(0, 27 * O, 2 * J):
            end = min(k + 2 * J, 27 * O)
            out[:, k:end] = flat[k:end].T

    loads[0].wait()

    turned(w2, w2t)

    def spread(src, dst, t, i):
        wide = src[t, i].astype(F32)
        dst[t, i, 0:O] = moved_cols(wide, 1).astype(BF16)
        dst[t, i, O : 2 * O] = src[t, i]
        dst[t, i, 2 * O : 3 * O] = moved_cols(wide, -1).astype(BF16)

    def back(source, weight, out):
        @pl.loop(0, slabs // 2)
        def _(s):
            t, i = s // (R // 2), 2 * lax.rem(s, R // 2)
            windows = [
                jnp.concatenate([source[t + 2 - a, i + 2 - b], source[t + 2 - a, i + 3 - b]], 1)
                for a in range(3)
                for b in range(3)
            ]
            total = jnp.dot(weight[...], jnp.concatenate(windows, 0), preferred_element_type=F32)
            out[2 * s] = total[:, :J].astype(BF16)
            out[2 * s + 1] = total[:, J:].astype(BF16)

    arrive(g_plan)

    @pl.loop(0, 2 * F * (R + 2), unroll=4)
    def _(s):
        spread(g, gsh, s // (R + 2), lax.rem(s, R + 2))

    back(gsh, w2t, ga)
    scatter(1, ga, gain)
    loads[1].wait()

    for q in range(Z):
        w1c[q] = jnp.concatenate([w1[ab][:, q * C : (q + 1) * C] for ab in range(9)], 1)

    def forward(q, first=False, last=False):
        channels = chunk(q)

        @pl.loop(0, slabs // 2)
        def _(s):
            t, i = s // (R // 2), 2 * lax.rem(s, R // 2)
            windows = [
                jnp.concatenate([x[t + a, i + b, channels, :], x[t + a, i + b + 1, channels, :]], 1)
                for a in range(3)
                for b in range(3)
            ]
            total = jnp.dot(w1c[q], jnp.concatenate(windows, 0), preferred_element_type=F32)
            if not first:
                total += raw[s]
            if not last:
                raw[s] = total
                return
            for half in range(2):
                cols = total[:, half * J : (half + 1) * J]
                value = moved_cols(cols[0:O], -1) + cols[O : 2 * O] + moved_cols(cols[2 * O :], 1)
                pre[2 * s + half] = value
                act[2 * s + half, mine, :] = (value * jax.nn.sigmoid(value)).astype(BF16)

    before = z
    for k in range(Z - 1):
        q = gathered(0, k, x_block)
        depart(x_halo(q))
        if k == Z - 2:
            scatter_rest(1, ga, gain)
        arrive(x_halo(before))
        forward(before, first=k == 0)
        before = q
    turned(w1, w1t)
    arrive(x_halo(before))
    forward(before, last=True)

    scattered(1, ga, gain)
    gather(2, act_block)

    @pl.loop(0, slabs, unroll=4)
    def _(s):
        t, i = s // R, lax.rem(s, R)
        total = summed(ga, gain, s)
        value = pre[s]
        sig = jax.nn.sigmoid(value)
        gp[t, i + 1] = (total * sig * (1.0 + value * (1.0 - sig))).astype(BF16)

    gp_plan = halo_plan(gp, -1, pl.ds(0, C), gh_send.at[1], gh_recv.at[1])
    depart(gp_plan)

    @pl.loop(0, slabs, unroll=4)
    def _(s):
        spread(gp, gpsh, s // R, lax.rem(s, R) + 1)

    nt = (((1,), (1,)), ((), ()))

    def row_of(source, t0, i0):
        return jnp.concatenate([source[t0 + s // R, i0 + s % R] for s in range(slabs)], 1)

    my_rows = pl.ds(pl.multiple_of(h * part, part), part)

    def taps(a):
        return pl.ds(3 * a, 3)

    def to_pair(f, a, left_of, right_of):
        @pl.loop(0, 3)
        def _(b):
            value = lax.dot_general(left_of(a, b), right_of(a, b), nt, preferred_element_type=F32)
            left, right = value[:, :J], value[:, J:]
            town[f, 3 * a + b] = jnp.where(parity == 0, left, right)
            tsend[f, 3 * a + b] = jnp.where(parity == 0, right, left).astype(BF16)

        return send(remote(
            tsend.at[f, taps(a)], trecv.at[f, taps(a)], t_send.at[f, a], t_recv.at[f, a], {"tm": pair}
        ))

    def to_rows(f, a, copy):
        copy.wait_recv()

        @pl.loop(3 * a, 3 * a + 3, unroll=3)
        def _(ab):
            total = town[f, ab] + trecv[f, ab].astype(F32)
            hown[f, ab] = total
            hsend[f, ab] = total.astype(BF16)

        return [
            send(remote(
                hsend.at[f, taps(a), pl.ds(pl.multiple_of(lax.rem(h + d, H) * part, part), part), :],
                hrecv.at[f, d - 1, taps(a)],
                h_send.at[f, a, d - 1], h_recv.at[f, a, d - 1], hpeer(d),
            ))
            for d in range(1, H)
        ]

    def piece(f, a, row):
        return fin.at[f, parity, taps(a), pl.ds(pl.multiple_of(row * part, part), part), :]

    def relay(f, a, d):
        block = piece(f, a, lax.rem(h - d + H, H))
        return send(remote(block, block, p_send.at[f, a, d], p_recv.at[f, a, d], {"tm": pair}))

    def from_rows(f, a, copies):
        for copy in copies:
            copy.wait_recv()

        @pl.loop(3 * a, 3 * a + 3, unroll=3)
        def _(ab):
            total = hown[f, ab, my_rows, :]
            for d in range(1, H):
                total += hrecv[f, d - 1, ab].astype(F32)
            fin[f, parity, ab, my_rows, :] = total.astype(BF16)

        block = piece(f, a, h)
        copies = [
            send(remote(block, block, a_send.at[f, a, d - 1], a_recv.at[f, a, d - 1], hpeer(d)))
            for d in range(1, H)
        ]
        return copies, [relay(f, a, 0)]

    def to_other(f, a, state):
        copies, relays = state
        for d in range(1, H):
            copies[d - 1].wait_recv()
            relays.append(relay(f, a, d))
        return relays

    def first_left(a, b):
        return row_of(gpsh, 0, 1)

    def first_right(a, b):
        return row_of(x, a, b)

    def second_left(a, b):
        return row_of(gsh, 2 - a, 2 - b)

    def second_right(a, b):
        return jnp.concatenate([act[s] for s in range(slabs)], 1)

    one = [to_pair(0, a, first_left, first_right) for a in range(3)]
    one = [to_rows(0, a, one[a]) for a in range(3)]

    arrive(gp_plan)

    @pl.loop(0, F * (R + 2), unroll=4)
    def _(s):
        spread(gp, gpsh, F + s // (R + 2), lax.rem(s, R + 2))

    for t in range(F):
        for i in (0, R + 1):
            spread(gp, gpsh, t, i)
    back(gpsh, w1t, gf)
    one = [from_rows(0, a, one[a]) for a in range(3)]

    for k in range(Z - 1):
        gathered(2, k, act_block)
    scatter(3, gf, gfin)

    two = [to_pair(1, a, second_left, second_right) for a in range(3)]
    two = [to_rows(1, a, two[a]) for a in range(3)]
    scatter_rest(3, gf, gfin)
    one = [to_other(0, a, one[a]) for a in range(3)]
    two = [from_rows(1, a, two[a]) for a in range(3)]

    stores = []

    def store(f, a, relays, out):
        for copy in relays:
            copy.wait_recv()
        copy = pltpu.make_async_copy(fin.at[f, :, taps(a)], out.at[:, taps(a)], local.at[3 * f + a])
        copy.start()
        stores.append(copy)

    for a in range(3):
        store(0, a, one[a], g1_out)
    two = [to_other(1, a, two[a]) for a in range(3)]
    scattered(3, gf, gfin)

    @pl.loop(0, slabs, unroll=4)
    def _(s):
        gf_out[s // R, lax.rem(s, R)] = summed(gf, gfin, s).astype(BF16)

    for a in range(3):
        store(1, a, two[a], g2_out)

    for go, copy in pending:
        if go is None:
            copy.wait_send()
        else:
            pl.when(go)(copy.wait_send)
    for plan in [g_plan, gp_plan] + [x_halo(q) for q in range(Z)]:
        for go, _, copy in plan:
            pl.when(go)(copy.wait_send)
    for copy in stores:
        copy.wait()


def on_device(sizes, frames, grad_out, weight_one, weight_two):
    T, H, Z = sizes
    F, R, C, J = frames.shape
    CC, slabs, part = C * Z, F * R, 3 * C // H

    def taps_first(weight):
        return weight.transpose(1, 2, 3, 0, 4).reshape(9, 3 * C, CC)

    dma = pltpu.SemaphoreType.DMA
    ext = (2 * F, R + 2)
    scratch = [
        pltpu.VMEM((9, 3 * C, CC), BF16),
        pltpu.VMEM((9, 3 * C, CC), BF16),
        pltpu.VMEM((Z, 3 * C, 9 * C), BF16),
        pltpu.VMEM((slabs // 2, 3 * C, 2 * J), F32),
        pltpu.VMEM(ext + (CC, J), BF16),
        pltpu.VMEM(ext + (C, J), BF16),
        pltpu.VMEM(ext + (3 * C, J), BF16),
        pltpu.VMEM(ext + (C, J), BF16),
        pltpu.VMEM(ext + (3 * C, J), BF16),
        pltpu.VMEM((CC, 27 * C), BF16),
        pltpu.VMEM((CC, 27 * C), BF16),
        pltpu.VMEM((slabs, C, J), F32),
        pltpu.VMEM((slabs, CC, J), BF16),
        pltpu.VMEM((Z, slabs, C, J), BF16),
        pltpu.VMEM((slabs, CC, J), BF16),
        pltpu.VMEM((slabs, CC, J), BF16),
        pltpu.VMEM((Z, slabs, C, J), BF16),
        pltpu.VMEM((2, slabs, C, J), BF16),
        pltpu.VMEM((2, 9, 3 * C, CC // 2), F32),
        pltpu.VMEM((2, 9, 3 * C, CC // 2), BF16),
        pltpu.VMEM((2, 9, 3 * C, CC // 2), BF16),
        pltpu.VMEM((2, 9, 3 * C, CC // 2), F32),
        pltpu.VMEM((2, 9, 3 * C, CC // 2), BF16),
        pltpu.VMEM((2, H - 1, 9, part, CC // 2), BF16),
        pltpu.VMEM((2, 2, 9, 3 * C, CC // 2), BF16),
        dma((4, Z)), dma((4, Z)), dma((4, Z)), dma((4,)),
        dma((Z, HALO)), dma((Z, HALO)), dma((2, HALO)), dma((2, HALO)),
        dma((2, 3)), dma((2, 3)), dma((2, 3, H - 1)), dma((2, 3, H - 1)),
        dma((2, 3, H - 1)), dma((2, 3, H - 1)), dma((2, 3, H)), dma((2, 3, H)), dma((6,)),
    ]
    vmem = pl.BlockSpec(memory_space=pltpu.VMEM)
    hbm = pl.BlockSpec(memory_space=pl.ANY)
    grad_frames, one, two = pl.pallas_call(
        functools.partial(kernel, sizes),
        out_shape=(
            jax.ShapeDtypeStruct((F, R, C, J), BF16),
            jax.ShapeDtypeStruct((2, 9, 3 * C, CC // 2), BF16),
            jax.ShapeDtypeStruct((2, 9, 3 * C, CC // 2), BF16),
        ),
        in_specs=[hbm] * 4,
        out_specs=(vmem, hbm, hbm),
        scratch_shapes=scratch,
        compiler_params=pltpu.CompilerParams(
            collective_id=0, has_side_effects=True, vmem_limit_bytes=56 * 1024 * 1024
        ),
    )(frames, grad_out, taps_first(weight_one), taps_first(weight_two))

    def widened(cells_in, one_in, two_in, cells_out, one_out, two_out):
        cells_out[...] = cells_in[...]
        for narrow, wide in ((one_in, one_out), (two_in, two_out)):
            for half in range(2):
                wide[:, :, half * CC // 2 : (half + 1) * CC // 2] = narrow[half].astype(F32)

    cells = pl.BlockSpec((F, R, C, J), lambda a: (0, 0, 0, 0))
    narrow = pl.BlockSpec((2, 1, 3 * C, CC // 2), lambda a: (0, a, 0, 0))
    wide = pl.BlockSpec((1, 3 * C, CC), lambda a: (a, 0, 0))
    filters = jax.ShapeDtypeStruct((9, 3 * C, CC), F32)
    grad_frames, one, two = pl.pallas_call(
        widened,
        grid=(9,),
        out_shape=(jax.ShapeDtypeStruct((F, R, C, J), BF16), filters, filters),
        in_specs=[cells, narrow, narrow],
        out_specs=(cells, wide, wide),
        compiler_params=pltpu.CompilerParams(vmem_limit_bytes=56 * 1024 * 1024),
    )(grad_frames, one, two)

    def whole(grad):
        if T > 2:
            groups = [list(range(0, T, 2)), list(range(1, T, 2))]
            grad = lax.psum(grad, "tm", axis_index_groups=groups)
        return grad.reshape(3, 3, 3, C, CC).transpose(3, 0, 1, 2, 4)

    return grad_frames, whole(one), whole(two)


def solution(mesh):
    sizes = (mesh.shape["tm"], mesh.shape["height"], mesh.shape["chan"])
    cells = P("tm", "height", "chan", None)
    filters = P("chan", None, None, None, None)
    return jax.shard_map(
        functools.partial(on_device, sizes),
        mesh=mesh,
        in_specs=(cells, cells, filters, filters),
        out_specs=(cells, filters, filters),
        check_vma=False,
    )
```

```python
import functools

import jax
import jax.numpy as jnp
from jax import lax
from jax.experimental import pallas as pl
from jax.experimental.pallas import tpu as pltpu
from jax.sharding import PartitionSpec as P

BF16 = jnp.bfloat16
F32 = jnp.float32
MESH = pl.DeviceIdType.MESH
HALO = 5


def moved_cols(block, offset):
    lane = lax.broadcasted_iota(jnp.int32, block.shape, 1)
    cols = block.shape[1]
    if offset > 0:
        return jnp.where(lane == cols - 1, 0.0, pltpu.roll(block, cols - 1, 1))
    return jnp.where(lane == 0, 0.0, pltpu.roll(block, 1, 1))


def kernel(
    sizes,
    frames, gout, w1_in, w2_in,
    gf_out, g1_out, g2_out,
    w1, w2, x, g, gsh, gp, gpsh, w1t, w2t, pre, ga, gain, act, gf, gfin, via,
    town, tsend, trecv, hown, hsend, hrecv, fin,
    z_send, z_recv, zz_send, zz_recv, xh_send, xh_recv, gh_send, gh_recv,
    t_send, t_recv, h_send, h_recv, a_send, a_recv, p_send, p_recv, local,
):
    T, H, Z = sizes
    F, R, C, J = gf_out.shape
    CC = C * Z
    O = C
    slabs = F * R
    part = 3 * O // H
    FAR = 3 if Z == 4 else Z
    tm, h, z = lax.axis_index("tm"), lax.axis_index("height"), lax.axis_index("chan")
    pair = tm + 1 - 2 * lax.rem(tm, 2)
    parity = lax.rem(tm, 2)

    up, down = h > 0, h < H - 1
    has_prev, has_next = tm > 0, tm < T - 1

    def zpeer(d):
        return {"chan": lax.rem(z + d, Z)}

    def hpeer(d):
        return {"height": lax.rem(h + d, H)}

    both = jnp.logical_and

    loads = [
        pltpu.make_async_copy(w2_in, w2, local.at[0]),
        pltpu.make_async_copy(w1_in, w1, local.at[1]),
        pltpu.make_async_copy(
            frames,
            x.at[pl.ds(F, F), pl.ds(1, R), pl.ds(pl.multiple_of(z * C, C), C), :],
            local.at[4],
        ),
        pltpu.make_async_copy(gout, g.at[pl.ds(0, F), pl.ds(1, R)], local.at[5]),
    ]
    for k in (2, 3, 0, 1):
        loads[k].start()

    barrier = pltpu.get_barrier_semaphore()
    for d in range(1, Z):
        pl.semaphore_signal(barrier, inc=1, device_id=zpeer(d), device_id_type=MESH)
    for d in range(1, H):
        pl.semaphore_signal(barrier, inc=1, device_id=hpeer(d), device_id_type=MESH)
    for cond_t, dt in ((has_prev, -1), (has_next, 1)):
        @pl.when(cond_t)
        def _(dt=dt):
            pl.semaphore_signal(barrier, inc=1, device_id={"tm": tm + dt}, device_id_type=MESH)
        for cond_h, dh in ((up, -1), (down, 1)):
            @pl.when(jnp.logical_and(cond_t, cond_h))
            def _(dt=dt, dh=dh):
                pl.semaphore_signal(
                    barrier, inc=1, device_id={"tm": tm + dt, "height": h + dh}, device_id_type=MESH
                )
    def near(p):
        return both(z != p, jnp.abs(z - p) < FAR)

    def zero_edges(ext, dt):
        f0 = 0 if dt > 0 else F

        @pl.when(jnp.logical_not(has_prev if dt > 0 else has_next))
        def _():
            ext[f0 : f0 + F] = jnp.zeros((F,) + ext.shape[1:], ext.dtype)

        @pl.when(jnp.logical_not(up))
        def _():
            ext[:, 0] = jnp.zeros((2 * F,) + ext.shape[2:], ext.dtype)

        @pl.when(jnp.logical_not(down))
        def _():
            ext[:, R + 1] = jnp.zeros((2 * F,) + ext.shape[2:], ext.dtype)

    zero_edges(g, -1)
    zero_edges(gp, -1)
    zero_edges(x, 1)
    for dst in (gain, gfin):
        for q in range(Z):
            @pl.when(jnp.logical_not(near(q)))
            def _(dst=dst, q=q):
                dst[q] = jnp.zeros(dst.shape[1:], dst.dtype)

    def turned(weight, out):
        flat = weight[...].reshape(27 * O, CC)
        for k in range(0, 27 * O, 2 * J):
            end = min(k + 2 * J, 27 * O)
            out[:, k:end] = flat[k:end].T

    loads[0].wait()
    turned(w2, w2t)

    n_t = jnp.where(has_prev, 1, 0) + jnp.where(has_next, 1, 0)
    n_h = jnp.where(up, 1, 0) + jnp.where(down, 1, 0)
    pl.semaphore_wait(barrier, (Z - 1) + (H - 1) + n_t + n_t * n_h)

    pending = []

    def remote(src, dst, ssem, rsem, dev):
        return pltpu.make_async_remote_copy(
            src_ref=src, dst_ref=dst, send_sem=ssem, recv_sem=rsem, device_id=dev, device_id_type=MESH
        )

    def send(copy):
        copy.start()
        pending.append((None, copy))
        return copy

    def send_if(go, copy):
        pl.when(go)(copy.start)
        pending.append((go, copy))

    def halo_plan(ext, dt, chan_slice, ssems, rsems):
        o0, f0 = (F, 0) if dt > 0 else (0, F)
        to_t = has_next if dt > 0 else has_prev
        from_t = has_prev if dt > 0 else has_next

        def at(frame, row, rows):
            return ext.at[pl.ds(frame, F), pl.ds(row, rows), chan_slice, :]

        plan = [
            (to_t, from_t, at(o0, 1, R), at(f0, 1, R), {"tm": tm + dt}),
            (down, up, at(o0, R, 1), at(o0, 0, 1), {"height": h + 1}),
            (up, down, at(o0, 1, 1), at(o0, R + 1, 1), {"height": h - 1}),
            (
                both(to_t, down), both(from_t, up),
                at(o0, R, 1), at(f0, 0, 1), {"tm": tm + dt, "height": h + 1},
            ),
            (
                both(to_t, up), both(from_t, down),
                at(o0, 1, 1), at(f0, R + 1, 1), {"tm": tm + dt, "height": h - 1},
            ),
        ]
        return [
            (go, come, remote(src, dst, ssems.at[k], rsems.at[k], dev))
            for k, (go, come, src, dst, dev) in enumerate(plan)
        ]

    def depart(plan):
        for go, _, copy in plan:
            pl.when(go)(copy.start)

    def arrive(plan):
        for _, come, copy in plan:
            pl.when(come)(copy.wait_recv)

    def chunk(index):
        return pl.ds(pl.multiple_of(index * C, C), C)

    mine = chunk(z)

    def gather(phase, block):
        for p in sorted(range(Z), key=lambda p: abs(2 * p - Z + 1)):
            send_if(near(p), remote(
                block(z), block(z), z_send.at[phase, p], z_recv.at[phase, z], {"chan": p}
            ))

    def nearest(k):
        low = z < Z // 2
        side = jnp.where(low, z, Z - 1 - z)
        other = jnp.where(k < side, k, k + 1)
        return jnp.where(low, other, Z - 1 - other)

    def gathered(phase, k, block, unless=None):
        q = nearest(k)
        landed = remote(
            block(q), block(q), z_send.at[phase, q], z_recv.at[phase, q], zpeer(1)
        )
        if unless is None:
            landed.wait_recv()
        else:
            pl.when(jnp.logical_not(unless))(landed.wait_recv)
        if FAR < Z and unless is None:
            for go, dz in (
                (both(both(q < z, z < Z - 1), z + 1 - q >= FAR), 1),
                (both(both(q > z, z > 0), q + 1 - z >= FAR), -1),
            ):
                send_if(go, remote(
                    block(q), block(q), zz_send.at[phase, k], z_recv.at[phase, q], {"chan": z + dz}
                ))
        return q

    middle = both(z > 0, z < Z - 1)

    def forwarded(phase, block):
        if FAR < Z:
            q = nearest(Z - 2)

            @pl.when(middle)
            def _():
                remote(
                    block(q), block(q), z_send.at[phase, q], z_recv.at[phase, q], zpeer(1)
                ).wait_recv()

            for go, dz in ((both(middle, q < z), 1), (both(middle, q > z), -1)):
                send_if(go, remote(
                    block(q), block(q), zz_send.at[phase, 0], z_recv.at[phase, q], {"chan": z + dz}
                ))

    ends = (0, Z - 1) if FAR < Z else ()

    def takes(p):
        return z == (1 if p == Z - 1 else Z - 2)

    def passed(phase, src, p):
        dz = 1 if p == Z - 1 else -1
        return remote(
            src.at[:, pl.ds(p * C, C), :], via.at[phase // 2],
            zz_send.at[phase, 0], zz_recv.at[phase], {"chan": lax.rem(z + dz + Z, Z)},
        )

    def direct(phase, src, dst, p):
        return remote(
            src.at[:, pl.ds(p * C, C), :], dst.at[z], z_send.at[phase, p], z_recv.at[phase, z], {"chan": p}
        )

    def scatter(phase, src, dst):
        for p in ends:
            send_if(z == Z - 1 - p, passed(phase, src, p))
        for p in range(Z):
            go = both(near(p), jnp.logical_not(takes(p))) if p in ends else near(p)
            pl.when(go)(direct(phase, src, dst, p).start)

    def scatter_rest(phase, src, dst):
        for p in ends:
            @pl.when(takes(p))
            def _(p=p):
                passed(phase, src, p).wait_recv()
                rows = slice(p * C, p * C + C)
                src[:, rows, :] = (
                    src[:, rows, :].astype(F32) + via[phase // 2].astype(F32)
                ).astype(BF16)
                direct(phase, src, dst, p).start()
        for p in range(Z):
            pending.append((near(p), direct(phase, src, dst, p)))

    def scattered(phase, src, dst):
        for q in range(Z):
            pl.when(near(q))(remote(
                src.at[:, pl.ds(0, C), :], dst.at[q], z_send.at[phase, q], z_recv.at[phase, q], zpeer(1)
            ).wait_recv)

    def summed(src, dst, s):
        total = src[s, mine, :].astype(F32)
        for q in range(Z):
            total += dst[q, s].astype(F32)
        return total

    def x_block(q):
        return x.at[pl.ds(F, F), pl.ds(1, R), chunk(q), :]

    def act_block(q):
        return act.at[:, chunk(q), :]

    def x_halo(q):
        return halo_plan(x, 1, chunk(q), xh_send.at[q], xh_recv.at[q])

    loads[2].wait()
    gather(0, x_block)
    loads[3].wait()
    g_plan = halo_plan(g, -1, pl.ds(0, C), gh_send.at[0], gh_recv.at[0])
    depart(g_plan)
    depart(x_halo(z))

    def spread(src, dst, t, i):
        wide = src[t, i].astype(F32)
        dst[t, i, 0:O] = moved_cols(wide, 1).astype(BF16)
        dst[t, i, O : 2 * O] = src[t, i]
        dst[t, i, 2 * O : 3 * O] = moved_cols(wide, -1).astype(BF16)

    def back(source, weight, out):
        @pl.loop(0, slabs // 2)
        def _(s):
            t, i = s // (R // 2), 2 * lax.rem(s, R // 2)
            windows = [
                jnp.concatenate([source[t + 2 - a, i + 2 - b], source[t + 2 - a, i + 3 - b]], 1)
                for a in range(3)
                for b in range(3)
            ]
            total = jnp.dot(weight[...], jnp.concatenate(windows, 0), preferred_element_type=F32)
            out[2 * s] = total[:, :J].astype(BF16)
            out[2 * s + 1] = total[:, J:].astype(BF16)

    arrive(g_plan)

    @pl.loop(0, 2 * F * (R + 2), unroll=4)
    def _(s):
        spread(g, gsh, s // (R + 2), lax.rem(s, R + 2))

    back(gsh, w2t, ga)
    scatter(1, ga, gain)
    loads[1].wait()

    for k in range(Z - 1):
        depart(x_halo(gathered(0, k, x_block)))
    scatter_rest(1, ga, gain)

    turned(w1, w1t)

    for q in range(Z):
        arrive(x_halo(q))

    @pl.loop(0, slabs // 2)
    def _(s):
        t, i = s // (R // 2), 2 * lax.rem(s, R // 2)
        windows = [
            jnp.concatenate([x[t + a, i + b], x[t + a, i + b + 1]], 1)
            for a in range(3)
            for b in range(3)
        ]
        taps_of = jnp.concatenate([w1[ab] for ab in range(9)], 1)
        total = jnp.dot(taps_of, jnp.concatenate(windows, 0), preferred_element_type=F32)
        for half in range(2):
            cols = total[:, half * J : (half + 1) * J]
            value = moved_cols(cols[0:O], -1) + cols[O : 2 * O] + moved_cols(cols[2 * O :], 1)
            pre[2 * s + half] = value
            act[2 * s + half, mine, :] = (value * jax.nn.sigmoid(value)).astype(BF16)

    scattered(1, ga, gain)
    gather(2, act_block)

    @pl.loop(0, slabs, unroll=4)
    def _(s):
        t, i = s // R, lax.rem(s, R)
        total = summed(ga, gain, s)
        value = pre[s]
        sig = jax.nn.sigmoid(value)
        gp[t, i + 1] = (total * sig * (1.0 + value * (1.0 - sig))).astype(BF16)

    gp_plan = halo_plan(gp, -1, pl.ds(0, C), gh_send.at[1], gh_recv.at[1])
    depart(gp_plan)

    @pl.loop(0, slabs, unroll=4)
    def _(s):
        spread(gp, gpsh, s // R, lax.rem(s, R) + 1)

    nt = (((1,), (1,)), ((), ()))

    def row_of(source, t0, i0):
        return jnp.concatenate([source[t0 + s // R, i0 + s % R] for s in range(slabs)], 1)

    my_rows = pl.ds(pl.multiple_of(h * part, part), part)

    def taps(a):
        return pl.ds(3 * a, 3)

    def to_pair(f, a, left_of, right_of):
        @pl.loop(0, 3)
        def _(b):
            value = lax.dot_general(left_of(a, b), right_of(a, b), nt, preferred_element_type=F32)
            left, right = value[:, :J], value[:, J:]
            town[f, 3 * a + b] = jnp.where(parity == 0, left, right)
            tsend[f, 3 * a + b] = jnp.where(parity == 0, right, left).astype(BF16)

        return send(remote(
            tsend.at[f, taps(a)], trecv.at[f, taps(a)], t_send.at[f, a], t_recv.at[f, a], {"tm": pair}
        ))

    def to_rows(f, a, copy):
        copy.wait_recv()

        @pl.loop(3 * a, 3 * a + 3, unroll=3)
        def _(ab):
            total = town[f, ab] + trecv[f, ab].astype(F32)
            hown[f, ab] = total
            hsend[f, ab] = total.astype(BF16)

        return [
            send(remote(
                hsend.at[f, taps(a), pl.ds(pl.multiple_of(lax.rem(h + d, H) * part, part), part), :],
                hrecv.at[f, d - 1, taps(a)],
                h_send.at[f, a, d - 1], h_recv.at[f, a, d - 1], hpeer(d),
            ))
            for d in range(1, H)
        ]

    def piece(f, a, row):
        return fin.at[f, parity, taps(a), pl.ds(pl.multiple_of(row * part, part), part), :]

    def relay(f, a, d):
        block = piece(f, a, lax.rem(h - d + H, H))
        return send(remote(block, block, p_send.at[f, a, d], p_recv.at[f, a, d], {"tm": pair}))

    def from_rows(f, a, copies):
        for copy in copies:
            copy.wait_recv()

        @pl.loop(3 * a, 3 * a + 3, unroll=3)
        def _(ab):
            total = hown[f, ab, my_rows, :]
            for d in range(1, H):
                total += hrecv[f, d - 1, ab].astype(F32)
            fin[f, parity, ab, my_rows, :] = total.astype(BF16)

        block = piece(f, a, h)
        copies = [
            send(remote(block, block, a_send.at[f, a, d - 1], a_recv.at[f, a, d - 1], hpeer(d)))
            for d in range(1, H)
        ]
        return copies, [relay(f, a, 0)]

    def to_other(f, a, state):
        copies, relays = state
        for d in range(1, H):
            copies[d - 1].wait_recv()
            relays.append(relay(f, a, d))
        return relays

    def first_left(a, b):
        return row_of(gpsh, 0, 1)

    def first_right(a, b):
        return row_of(x, a, b)

    def second_left(a, b):
        return row_of(gsh, 2 - a, 2 - b)

    def second_right(a, b):
        return jnp.concatenate([act[s] for s in range(slabs)], 1)

    one = [to_pair(0, a, first_left, first_right) for a in range(3)]
    forwarded(2, act_block)
    one = [to_rows(0, a, one[a]) for a in range(3)]

    arrive(gp_plan)

    @pl.loop(0, F * (R + 2), unroll=4)
    def _(s):
        spread(gp, gpsh, F + s // (R + 2), lax.rem(s, R + 2))

    for t in range(F):
        for i in (0, R + 1):
            spread(gp, gpsh, t, i)
    back(gpsh, w1t, gf)
    one = [from_rows(0, a, one[a]) for a in range(3)]

    for k in range(Z - 1):
        gathered(2, k, act_block, unless=both(middle, k == Z - 2) if FAR < Z else both(z < 0, z > 0))
    scatter(3, gf, gfin)

    two = [to_pair(1, a, second_left, second_right) for a in range(3)]
    two = [to_rows(1, a, two[a]) for a in range(3)]
    scatter_rest(3, gf, gfin)
    one = [to_other(0, a, one[a]) for a in range(3)]
    two = [from_rows(1, a, two[a]) for a in range(3)]

    stores = []

    def store(f, a, relays, out):
        for copy in relays:
            copy.wait_recv()
        copy = pltpu.make_async_copy(fin.at[f, :, taps(a)], out.at[:, taps(a)], local.at[3 * f + a])
        copy.start()
        stores.append(copy)

    for a in range(3):
        store(0, a, one[a], g1_out)
    two = [to_other(1, a, two[a]) for a in range(3)]
    scattered(3, gf, gfin)

    @pl.loop(0, slabs, unroll=4)
    def _(s):
        gf_out[s // R, lax.rem(s, R)] = summed(gf, gfin, s).astype(BF16)

    for a in range(3):
        store(1, a, two[a], g2_out)

    for go, copy in pending:
        if go is None:
            copy.wait_send()
        else:
            pl.when(go)(copy.wait_send)
    for plan in [g_plan, gp_plan] + [x_halo(q) for q in range(Z)]:
        for go, _, copy in plan:
            pl.when(go)(copy.wait_send)
    for copy in stores:
        copy.wait()


def on_device(sizes, frames, grad_out, weight_one, weight_two):
    T, H, Z = sizes
    F, R, C, J = frames.shape
    CC, slabs, part = C * Z, F * R, 3 * C // H

    def taps_first(weight):
        return weight.transpose(1, 2, 3, 0, 4).reshape(9, 3 * C, CC)

    dma = pltpu.SemaphoreType.DMA
    ext = (2 * F, R + 2)
    scratch = [
        pltpu.VMEM((9, 3 * C, CC), BF16),
        pltpu.VMEM((9, 3 * C, CC), BF16),
        pltpu.VMEM(ext + (CC, J), BF16),
        pltpu.VMEM(ext + (C, J), BF16),
        pltpu.VMEM(ext + (3 * C, J), BF16),
        pltpu.VMEM(ext + (C, J), BF16),
        pltpu.VMEM(ext + (3 * C, J), BF16),
        pltpu.VMEM((CC, 27 * C), BF16),
        pltpu.VMEM((CC, 27 * C), BF16),
        pltpu.VMEM((slabs, C, J), F32),
        pltpu.VMEM((slabs, CC, J), BF16),
        pltpu.VMEM((Z, slabs, C, J), BF16),
        pltpu.VMEM((slabs, CC, J), BF16),
        pltpu.VMEM((slabs, CC, J), BF16),
        pltpu.VMEM((Z, slabs, C, J), BF16),
        pltpu.VMEM((2, slabs, C, J), BF16),
        pltpu.VMEM((2, 9, 3 * C, CC // 2), F32),
        pltpu.VMEM((2, 9, 3 * C, CC // 2), BF16),
        pltpu.VMEM((2, 9, 3 * C, CC // 2), BF16),
        pltpu.VMEM((2, 9, 3 * C, CC // 2), F32),
        pltpu.VMEM((2, 9, 3 * C, CC // 2), BF16),
        pltpu.VMEM((2, H - 1, 9, part, CC // 2), BF16),
        pltpu.VMEM((2, 2, 9, 3 * C, CC // 2), BF16),
        dma((4, Z)), dma((4, Z)), dma((4, Z)), dma((4,)),
        dma((Z, HALO)), dma((Z, HALO)), dma((2, HALO)), dma((2, HALO)),
        dma((2, 3)), dma((2, 3)), dma((2, 3, H - 1)), dma((2, 3, H - 1)),
        dma((2, 3, H - 1)), dma((2, 3, H - 1)), dma((2, 3, H)), dma((2, 3, H)), dma((6,)),
    ]
    vmem = pl.BlockSpec(memory_space=pltpu.VMEM)
    hbm = pl.BlockSpec(memory_space=pl.ANY)
    grad_frames, one, two = pl.pallas_call(
        functools.partial(kernel, sizes),
        out_shape=(
            jax.ShapeDtypeStruct((F, R, C, J), BF16),
            jax.ShapeDtypeStruct((2, 9, 3 * C, CC // 2), BF16),
            jax.ShapeDtypeStruct((2, 9, 3 * C, CC // 2), BF16),
        ),
        in_specs=[hbm] * 4,
        out_specs=(vmem, hbm, hbm),
        scratch_shapes=scratch,
        compiler_params=pltpu.CompilerParams(
            collective_id=0, has_side_effects=True, vmem_limit_bytes=56 * 1024 * 1024
        ),
    )(frames, grad_out, taps_first(weight_one), taps_first(weight_two))

    narrow, wide = (2, 9, 3 * C, CC // 2), (9, 3 * C, CC)

    def widened(
        cells_in, one_in, two_in, cells_out, one_out, two_out,
        cells, narrow_one, narrow_two, wide_one, wide_two, arrived, left,
    ):
        both = ((one_in, narrow_one, wide_one, one_out), (two_in, narrow_two, wide_two, two_out))
        fetch = []
        for f, (source, near, _, _) in enumerate(both):
            for a in range(3):
                taps = pl.ds(3 * a, 3)
                fetch.append(pltpu.make_async_copy(source.at[:, taps], near.at[:, taps], arrived.at[f, a]))
        fetch.append(pltpu.make_async_copy(cells_in, cells, arrived.at[2, 0]))
        for copy in fetch:
            copy.start()
        stores = []
        for f, (_, near, far, out) in enumerate(both):
            for a in range(3):
                fetch[3 * f + a].wait()
                for ab in range(3 * a, 3 * a + 3):
                    for half in range(2):
                        far[ab, :, half * CC // 2 : (half + 1) * CC // 2] = near[half, ab].astype(F32)
                taps = pl.ds(3 * a, 3)
                stores.append(pltpu.make_async_copy(far.at[taps], out.at[taps], left.at[f, a]))
                stores[-1].start()
        fetch[6].wait()
        stores.append(pltpu.make_async_copy(cells, cells_out, left.at[2, 0]))
        stores[-1].start()
        for copy in stores:
            copy.wait()

    filters = jax.ShapeDtypeStruct(wide, F32)
    grad_frames, one, two = pl.pallas_call(
        widened,
        out_shape=(jax.ShapeDtypeStruct((F, R, C, J), BF16), filters, filters),
        in_specs=[hbm] * 3,
        out_specs=(hbm,) * 3,
        scratch_shapes=[
            pltpu.VMEM((F, R, C, J), BF16), pltpu.VMEM(narrow, BF16), pltpu.VMEM(narrow, BF16),
            pltpu.VMEM(wide, F32), pltpu.VMEM(wide, F32), dma((3, 3)), dma((3, 3)),
        ],
        compiler_params=pltpu.CompilerParams(vmem_limit_bytes=56 * 1024 * 1024),
    )(grad_frames, one, two)

    def whole(grad):
        if T > 2:
            groups = [list(range(0, T, 2)), list(range(1, T, 2))]
            grad = lax.psum(grad, "tm", axis_index_groups=groups)
        return grad.reshape(3, 3, 3, C, CC).transpose(3, 0, 1, 2, 4)

    return grad_frames, whole(one), whole(two)


def solution(mesh):
    sizes = (mesh.shape["tm"], mesh.shape["height"], mesh.shape["chan"])
    cells = P("tm", "height", "chan", None)
    filters = P("chan", None, None, None, None)
    return jax.shard_map(
        functools.partial(on_device, sizes),
        mesh=mesh,
        in_specs=(cells, cells, filters, filters),
        out_specs=(cells, filters, filters),
        check_vma=False,
    )
```

```python
import functools

import jax
import jax.numpy as jnp
from jax import lax
from jax.experimental import pallas as pl
from jax.experimental.pallas import tpu as pltpu
from jax.sharding import PartitionSpec as P

BF16 = jnp.bfloat16
F32 = jnp.float32
MESH = pl.DeviceIdType.MESH
HALO = 5


def moved_cols(block, offset):
    lane = lax.broadcasted_iota(jnp.int32, block.shape, 1)
    cols = block.shape[1]
    if offset > 0:
        return jnp.where(lane == cols - 1, 0.0, pltpu.roll(block, cols - 1, 1))
    return jnp.where(lane == 0, 0.0, pltpu.roll(block, 1, 1))


def kernel(
    sizes,
    frames, gout, w1_in, w2_in,
    gf_out, g1_out, g2_out,
    w1, w2, x, g, gsh, gp, gpsh, w1t, w2t, pre, ga, gain, act, gf, gfin, via,
    town, tsend, trecv, hown, hsend, hrecv, fin,
    z_send, z_recv, zz_send, zz_recv, xh_send, xh_recv, gh_send, gh_recv,
    t_send, t_recv, h_send, h_recv, a_send, a_recv, p_send, p_recv, local,
):
    T, H, Z = sizes
    F, R, C, J = gf_out.shape
    CC = C * Z
    O = C
    slabs = F * R
    part = 3 * O // H
    FAR = 3 if Z == 4 else Z
    tm, h, z = lax.axis_index("tm"), lax.axis_index("height"), lax.axis_index("chan")
    pair = tm + 1 - 2 * lax.rem(tm, 2)
    parity = lax.rem(tm, 2)

    up, down = h > 0, h < H - 1
    has_prev, has_next = tm > 0, tm < T - 1

    def zpeer(d):
        return {"chan": lax.rem(z + d, Z)}

    def hpeer(d):
        return {"height": lax.rem(h + d, H)}

    both = jnp.logical_and

    loads = [
        pltpu.make_async_copy(w2_in, w2, local.at[0]),
        pltpu.make_async_copy(w1_in, w1, local.at[1]),
        pltpu.make_async_copy(
            frames,
            x.at[pl.ds(F, F), pl.ds(1, R), pl.ds(pl.multiple_of(z * C, C), C), :],
            local.at[4],
        ),
        pltpu.make_async_copy(gout, g.at[pl.ds(0, F), pl.ds(1, R)], local.at[5]),
    ]
    for k in (2, 3, 0, 1):
        loads[k].start()

    barrier = pltpu.get_barrier_semaphore()
    for d in range(1, Z):
        pl.semaphore_signal(barrier, inc=1, device_id=zpeer(d), device_id_type=MESH)
    for d in range(1, H):
        pl.semaphore_signal(barrier, inc=1, device_id=hpeer(d), device_id_type=MESH)
    for cond_t, dt in ((has_prev, -1), (has_next, 1)):
        @pl.when(cond_t)
        def _(dt=dt):
            pl.semaphore_signal(barrier, inc=1, device_id={"tm": tm + dt}, device_id_type=MESH)
        for cond_h, dh in ((up, -1), (down, 1)):
            @pl.when(jnp.logical_and(cond_t, cond_h))
            def _(dt=dt, dh=dh):
                pl.semaphore_signal(
                    barrier, inc=1, device_id={"tm": tm + dt, "height": h + dh}, device_id_type=MESH
                )
    def near(p):
        return both(z != p, jnp.abs(z - p) < FAR)

    def zero_edges(ext, dt):
        f0 = 0 if dt > 0 else F

        @pl.when(jnp.logical_not(has_prev if dt > 0 else has_next))
        def _():
            ext[f0 : f0 + F] = jnp.zeros((F,) + ext.shape[1:], ext.dtype)

        @pl.when(jnp.logical_not(up))
        def _():
            ext[:, 0] = jnp.zeros((2 * F,) + ext.shape[2:], ext.dtype)

        @pl.when(jnp.logical_not(down))
        def _():
            ext[:, R + 1] = jnp.zeros((2 * F,) + ext.shape[2:], ext.dtype)

    zero_edges(g, -1)
    zero_edges(gp, -1)
    zero_edges(x, 1)
    for dst in (gain, gfin):
        for q in range(Z):
            @pl.when(jnp.logical_not(near(q)))
            def _(dst=dst, q=q):
                dst[q] = jnp.zeros(dst.shape[1:], dst.dtype)

    def turned(weight, out):
        flat = weight[...].reshape(27 * O, CC)
        for k in range(0, 27 * O, 2 * J):
            end = min(k + 2 * J, 27 * O)
            out[:, k:end] = flat[k:end].T

    loads[0].wait()
    turned(w2, w2t)

    n_t = jnp.where(has_prev, 1, 0) + jnp.where(has_next, 1, 0)
    n_h = jnp.where(up, 1, 0) + jnp.where(down, 1, 0)
    pl.semaphore_wait(barrier, (Z - 1) + (H - 1) + n_t + n_t * n_h)

    pending = []

    def remote(src, dst, ssem, rsem, dev):
        return pltpu.make_async_remote_copy(
            src_ref=src, dst_ref=dst, send_sem=ssem, recv_sem=rsem, device_id=dev, device_id_type=MESH
        )

    def send(copy):
        copy.start()
        pending.append((None, copy))
        return copy

    def send_if(go, copy):
        pl.when(go)(copy.start)
        pending.append((go, copy))

    def halo_plan(ext, dt, chan_slice, ssems, rsems):
        o0, f0 = (F, 0) if dt > 0 else (0, F)
        to_t = has_next if dt > 0 else has_prev
        from_t = has_prev if dt > 0 else has_next

        def at(frame, row, rows):
            return ext.at[pl.ds(frame, F), pl.ds(row, rows), chan_slice, :]

        plan = [
            (to_t, from_t, at(o0, 1, R), at(f0, 1, R), {"tm": tm + dt}),
            (down, up, at(o0, R, 1), at(o0, 0, 1), {"height": h + 1}),
            (up, down, at(o0, 1, 1), at(o0, R + 1, 1), {"height": h - 1}),
            (
                both(to_t, down), both(from_t, up),
                at(o0, R, 1), at(f0, 0, 1), {"tm": tm + dt, "height": h + 1},
            ),
            (
                both(to_t, up), both(from_t, down),
                at(o0, 1, 1), at(f0, R + 1, 1), {"tm": tm + dt, "height": h - 1},
            ),
        ]
        return [
            (go, come, remote(src, dst, ssems.at[k], rsems.at[k], dev))
            for k, (go, come, src, dst, dev) in enumerate(plan)
        ]

    def depart(plan):
        for go, _, copy in plan:
            pl.when(go)(copy.start)

    def arrive(plan):
        for _, come, copy in plan:
            pl.when(come)(copy.wait_recv)

    def chunk(index):
        return pl.ds(pl.multiple_of(index * C, C), C)

    mine = chunk(z)

    def gather(phase, block):
        for p in sorted(range(Z), key=lambda p: abs(2 * p - Z + 1)):
            send_if(near(p), remote(
                block(z), block(z), z_send.at[phase, p], z_recv.at[phase, z], {"chan": p}
            ))

    def nearest(k):
        low = z < Z // 2
        side = jnp.where(low, z, Z - 1 - z)
        other = jnp.where(k < side, k, k + 1)
        return jnp.where(low, other, Z - 1 - other)

    def gathered(phase, k, block, unless=None):
        q = nearest(k)
        landed = remote(
            block(q), block(q), z_send.at[phase, q], z_recv.at[phase, q], zpeer(1)
        )
        if unless is None:
            landed.wait_recv()
        else:
            pl.when(jnp.logical_not(unless))(landed.wait_recv)
        if FAR < Z and unless is None:
            for go, dz in (
                (both(both(q < z, z < Z - 1), z + 1 - q >= FAR), 1),
                (both(both(q > z, z > 0), q + 1 - z >= FAR), -1),
            ):
                send_if(go, remote(
                    block(q), block(q), zz_send.at[phase, k], z_recv.at[phase, q], {"chan": z + dz}
                ))
        return q

    middle = both(z > 0, z < Z - 1)

    def forwarded(phase, block):
        if FAR < Z:
            q = nearest(Z - 2)

            @pl.when(middle)
            def _():
                remote(
                    block(q), block(q), z_send.at[phase, q], z_recv.at[phase, q], zpeer(1)
                ).wait_recv()

            for go, dz in ((both(middle, q < z), 1), (both(middle, q > z), -1)):
                send_if(go, remote(
                    block(q), block(q), zz_send.at[phase, 0], z_recv.at[phase, q], {"chan": z + dz}
                ))

    ends = (0, Z - 1) if FAR < Z else ()

    def takes(p):
        return z == (1 if p == Z - 1 else Z - 2)

    def passed(phase, src, p):
        dz = 1 if p == Z - 1 else -1
        return remote(
            src.at[:, pl.ds(p * C, C), :], via.at[phase // 2],
            zz_send.at[phase, 0], zz_recv.at[phase], {"chan": lax.rem(z + dz + Z, Z)},
        )

    def direct(phase, src, dst, p):
        return remote(
            src.at[:, pl.ds(p * C, C), :], dst.at[z], z_send.at[phase, p], z_recv.at[phase, z], {"chan": p}
        )

    def scatter(phase, src, dst, only=None):
        for p in ends:
            if only is not middle:
                send_if(z == Z - 1 - p, passed(phase, src, p))
        for p in range(Z):
            go = both(near(p), jnp.logical_not(takes(p))) if p in ends else near(p)
            go = go if only is None else both(go, only)
            pl.when(go)(direct(phase, src, dst, p).start)

    def scatter_rest(phase, src, dst):
        for p in ends:
            @pl.when(takes(p))
            def _(p=p):
                passed(phase, src, p).wait_recv()
                rows = slice(p * C, p * C + C)
                src[:, rows, :] = (
                    src[:, rows, :].astype(F32) + via[phase // 2].astype(F32)
                ).astype(BF16)
                direct(phase, src, dst, p).start()
        for p in range(Z):
            pending.append((near(p), direct(phase, src, dst, p)))

    def scattered(phase, src, dst):
        for q in range(Z):
            pl.when(near(q))(remote(
                src.at[:, pl.ds(0, C), :], dst.at[q], z_send.at[phase, q], z_recv.at[phase, q], zpeer(1)
            ).wait_recv)

    def summed(src, dst, s):
        total = src[s, mine, :].astype(F32)
        for q in range(Z):
            total += dst[q, s].astype(F32)
        return total

    def x_block(q):
        return x.at[pl.ds(F, F), pl.ds(1, R), chunk(q), :]

    def act_block(q):
        return act.at[:, chunk(q), :]

    def x_halo(q):
        return halo_plan(x, 1, chunk(q), xh_send.at[q], xh_recv.at[q])

    loads[2].wait()
    gather(0, x_block)
    loads[3].wait()
    g_plan = halo_plan(g, -1, pl.ds(0, C), gh_send.at[0], gh_recv.at[0])
    depart(g_plan)
    depart(x_halo(z))

    def spread(src, dst, t, i):
        wide = src[t, i].astype(F32)
        dst[t, i, 0:O] = moved_cols(wide, 1).astype(BF16)
        dst[t, i, O : 2 * O] = src[t, i]
        dst[t, i, 2 * O : 3 * O] = moved_cols(wide, -1).astype(BF16)

    def back(source, weight, out):
        @pl.loop(0, slabs // 2)
        def _(s):
            t, i = s // (R // 2), 2 * lax.rem(s, R // 2)
            windows = [
                jnp.concatenate([source[t + 2 - a, i + 2 - b], source[t + 2 - a, i + 3 - b]], 1)
                for a in range(3)
                for b in range(3)
            ]
            total = jnp.dot(weight[...], jnp.concatenate(windows, 0), preferred_element_type=F32)
            out[2 * s] = total[:, :J].astype(BF16)
            out[2 * s + 1] = total[:, J:].astype(BF16)

    arrive(g_plan)

    @pl.loop(0, 2 * F * (R + 2), unroll=4)
    def _(s):
        spread(g, gsh, s // (R + 2), lax.rem(s, R + 2))

    back(gsh, w2t, ga)
    scatter(1, ga, gain)
    loads[1].wait()

    for k in range(Z - 1):
        depart(x_halo(gathered(0, k, x_block)))
    scatter_rest(1, ga, gain)

    turned(w1, w1t)

    for q in range(Z):
        arrive(x_halo(q))

    @pl.loop(0, slabs // 2)
    def _(s):
        t, i = s // (R // 2), 2 * lax.rem(s, R // 2)
        windows = [
            jnp.concatenate([x[t + a, i + b], x[t + a, i + b + 1]], 1)
            for a in range(3)
            for b in range(3)
        ]
        taps_of = jnp.concatenate([w1[ab] for ab in range(9)], 1)
        total = jnp.dot(taps_of, jnp.concatenate(windows, 0), preferred_element_type=F32)
        for half in range(2):
            cols = total[:, half * J : (half + 1) * J]
            value = moved_cols(cols[0:O], -1) + cols[O : 2 * O] + moved_cols(cols[2 * O :], 1)
            pre[2 * s + half] = value
            act[2 * s + half, mine, :] = (value * jax.nn.sigmoid(value)).astype(BF16)

    gather(2, act_block)
    scattered(1, ga, gain)

    @pl.loop(0, slabs, unroll=4)
    def _(s):
        t, i = s // R, lax.rem(s, R)
        total = summed(ga, gain, s)
        value = pre[s]
        sig = jax.nn.sigmoid(value)
        gp[t, i + 1] = (total * sig * (1.0 + value * (1.0 - sig))).astype(BF16)

    gp_plan = halo_plan(gp, -1, pl.ds(0, C), gh_send.at[1], gh_recv.at[1])
    depart(gp_plan)

    @pl.loop(0, slabs, unroll=4)
    def _(s):
        spread(gp, gpsh, s // R, lax.rem(s, R) + 1)

    nt = (((1,), (1,)), ((), ()))

    def row_of(source, t0, i0):
        return jnp.concatenate([source[t0 + s // R, i0 + s % R] for s in range(slabs)], 1)

    my_rows = pl.ds(pl.multiple_of(h * part, part), part)

    def taps(a):
        return pl.ds(3 * a, 3)

    def to_pair(f, a, values):
        for b, value in enumerate(values):
            left, right = value[:, :J], value[:, J:]
            town[f, 3 * a + b] = jnp.where(parity == 0, left, right)
            tsend[f, 3 * a + b] = jnp.where(parity == 0, right, left).astype(BF16)

        return send(remote(
            tsend.at[f, taps(a)], trecv.at[f, taps(a)], t_send.at[f, a], t_recv.at[f, a], {"tm": pair}
        ))

    def to_rows(f, a, copy):
        copy.wait_recv()

        @pl.loop(3 * a, 3 * a + 3, unroll=3)
        def _(ab):
            total = town[f, ab] + trecv[f, ab].astype(F32)
            hown[f, ab] = total
            hsend[f, ab] = total.astype(BF16)

        return [
            send(remote(
                hsend.at[f, taps(a), pl.ds(pl.multiple_of(lax.rem(h + d, H) * part, part), part), :],
                hrecv.at[f, d - 1, taps(a)],
                h_send.at[f, a, d - 1], h_recv.at[f, a, d - 1], hpeer(d),
            ))
            for d in range(1, H)
        ]

    def piece(f, a, row):
        return fin.at[f, parity, taps(a), pl.ds(pl.multiple_of(row * part, part), part), :]

    def relay(f, a, d):
        block = piece(f, a, lax.rem(h - d + H, H))
        return send(remote(block, block, p_send.at[f, a, d], p_recv.at[f, a, d], {"tm": pair}))

    def from_rows(f, a, copies):
        for copy in copies:
            copy.wait_recv()

        @pl.loop(3 * a, 3 * a + 3, unroll=3)
        def _(ab):
            total = hown[f, ab, my_rows, :]
            for d in range(1, H):
                total += hrecv[f, d - 1, ab].astype(F32)
            fin[f, parity, ab, my_rows, :] = total.astype(BF16)

        block = piece(f, a, h)
        copies = [
            send(remote(block, block, a_send.at[f, a, d - 1], a_recv.at[f, a, d - 1], hpeer(d)))
            for d in range(1, H)
        ]
        return copies, [relay(f, a, 0)]

    def to_other(f, a, state):
        copies, relays = state
        for d in range(1, H):
            copies[d - 1].wait_recv()
            relays.append(relay(f, a, d))
        return relays

    def first_taps(a):
        left = row_of(gpsh, 0, 1)
        return [
            lax.dot_general(left, row_of(x, a, b), nt, preferred_element_type=F32) for b in range(3)
        ]

    def second_taps(a):
        left = jnp.concatenate([row_of(gsh, 2 - a, 2 - b) for b in range(3)], 0)
        right = jnp.concatenate([act[s] for s in range(slabs)], 1)
        value = lax.dot_general(left, right, nt, preferred_element_type=F32)
        return [value[b * 3 * O : (b + 1) * 3 * O] for b in range(3)]

    one = [to_pair(0, a, first_taps(a)) for a in range(3)]
    one = [to_rows(0, a, one[a]) for a in range(3)]
    forwarded(2, act_block)

    arrive(gp_plan)

    @pl.loop(0, F * (R + 2), unroll=4)
    def _(s):
        spread(gp, gpsh, F + s // (R + 2), lax.rem(s, R + 2))

    for t in range(F):
        for i in (0, R + 1):
            spread(gp, gpsh, t, i)
    back(gpsh, w1t, gf)
    scatter(3, gf, gfin, only=jnp.logical_not(middle))
    one = [from_rows(0, a, one[a]) for a in range(3)]

    for k in range(Z - 1):
        gathered(2, k, act_block, unless=both(middle, k == Z - 2) if FAR < Z else both(z < 0, z > 0))
    scatter(3, gf, gfin, only=middle)

    two = [to_pair(1, a, second_taps(a)) for a in range(3)]
    two = [to_rows(1, a, two[a]) for a in range(3)]
    one = [to_other(0, a, one[a]) for a in range(3)]
    two = [from_rows(1, a, two[a]) for a in range(3)]
    scatter_rest(3, gf, gfin)

    stores = []

    def store(f, a, relays, out):
        for copy in relays:
            copy.wait_recv()
        copy = pltpu.make_async_copy(fin.at[f, :, taps(a)], out.at[:, taps(a)], local.at[3 * f + a])
        copy.start()
        stores.append(copy)

    for a in range(3):
        store(0, a, one[a], g1_out)
    two = [to_other(1, a, two[a]) for a in range(3)]
    scattered(3, gf, gfin)

    @pl.loop(0, slabs, unroll=4)
    def _(s):
        gf_out[s // R, lax.rem(s, R)] = summed(gf, gfin, s).astype(BF16)

    for a in range(3):
        store(1, a, two[a], g2_out)

    for go, copy in pending:
        if go is None:
            copy.wait_send()
        else:
            pl.when(go)(copy.wait_send)
    for plan in [g_plan, gp_plan] + [x_halo(q) for q in range(Z)]:
        for go, _, copy in plan:
            pl.when(go)(copy.wait_send)
    for copy in stores:
        copy.wait()


def on_device(sizes, frames, grad_out, weight_one, weight_two):
    T, H, Z = sizes
    F, R, C, J = frames.shape
    CC, slabs, part = C * Z, F * R, 3 * C // H

    def taps_first(weight):
        return weight.transpose(1, 2, 3, 0, 4).reshape(9, 3 * C, CC)

    dma = pltpu.SemaphoreType.DMA
    ext = (2 * F, R + 2)
    scratch = [
        pltpu.VMEM((9, 3 * C, CC), BF16),
        pltpu.VMEM((9, 3 * C, CC), BF16),
        pltpu.VMEM(ext + (CC, J), BF16),
        pltpu.VMEM(ext + (C, J), BF16),
        pltpu.VMEM(ext + (3 * C, J), BF16),
        pltpu.VMEM(ext + (C, J), BF16),
        pltpu.VMEM(ext + (3 * C, J), BF16),
        pltpu.VMEM((CC, 27 * C), BF16),
        pltpu.VMEM((CC, 27 * C), BF16),
        pltpu.VMEM((slabs, C, J), F32),
        pltpu.VMEM((slabs, CC, J), BF16),
        pltpu.VMEM((Z, slabs, C, J), BF16),
        pltpu.VMEM((slabs, CC, J), BF16),
        pltpu.VMEM((slabs, CC, J), BF16),
        pltpu.VMEM((Z, slabs, C, J), BF16),
        pltpu.VMEM((2, slabs, C, J), BF16),
        pltpu.VMEM((2, 9, 3 * C, CC // 2), F32),
        pltpu.VMEM((2, 9, 3 * C, CC // 2), BF16),
        pltpu.VMEM((2, 9, 3 * C, CC // 2), BF16),
        pltpu.VMEM((2, 9, 3 * C, CC // 2), F32),
        pltpu.VMEM((2, 9, 3 * C, CC // 2), BF16),
        pltpu.VMEM((2, H - 1, 9, part, CC // 2), BF16),
        pltpu.VMEM((2, 2, 9, 3 * C, CC // 2), BF16),
        dma((4, Z)), dma((4, Z)), dma((4, Z)), dma((4,)),
        dma((Z, HALO)), dma((Z, HALO)), dma((2, HALO)), dma((2, HALO)),
        dma((2, 3)), dma((2, 3)), dma((2, 3, H - 1)), dma((2, 3, H - 1)),
        dma((2, 3, H - 1)), dma((2, 3, H - 1)), dma((2, 3, H)), dma((2, 3, H)), dma((6,)),
    ]
    vmem = pl.BlockSpec(memory_space=pltpu.VMEM)
    hbm = pl.BlockSpec(memory_space=pl.ANY)
    grad_frames, one, two = pl.pallas_call(
        functools.partial(kernel, sizes),
        out_shape=(
            jax.ShapeDtypeStruct((F, R, C, J), BF16),
            jax.ShapeDtypeStruct((2, 9, 3 * C, CC // 2), BF16),
            jax.ShapeDtypeStruct((2, 9, 3 * C, CC // 2), BF16),
        ),
        in_specs=[hbm] * 4,
        out_specs=(vmem, hbm, hbm),
        scratch_shapes=scratch,
        compiler_params=pltpu.CompilerParams(
            collective_id=0, has_side_effects=True, vmem_limit_bytes=56 * 1024 * 1024
        ),
    )(frames, grad_out, taps_first(weight_one), taps_first(weight_two))

    narrow, wide = (2, 9, 3 * C, CC // 2), (9, 3 * C, CC)

    def widened(
        cells_in, one_in, two_in, cells_out, one_out, two_out,
        cells, narrow_one, narrow_two, wide_one, wide_two, arrived, left,
    ):
        both = ((one_in, narrow_one, wide_one, one_out), (two_in, narrow_two, wide_two, two_out))
        fetch = []
        for f, (source, near, _, _) in enumerate(both):
            for a in range(3):
                taps = pl.ds(3 * a, 3)
                fetch.append(pltpu.make_async_copy(source.at[:, taps], near.at[:, taps], arrived.at[f, a]))
        fetch.append(pltpu.make_async_copy(cells_in, cells, arrived.at[2, 0]))
        for copy in fetch:
            copy.start()
        stores = []
        for f, (_, near, far, out) in enumerate(both):
            for a in range(3):
                fetch[3 * f + a].wait()
                for ab in range(3 * a, 3 * a + 3):
                    for half in range(2):
                        far[ab, :, half * CC // 2 : (half + 1) * CC // 2] = near[half, ab].astype(F32)
                taps = pl.ds(3 * a, 3)
                stores.append(pltpu.make_async_copy(far.at[taps], out.at[taps], left.at[f, a]))
                stores[-1].start()
        fetch[6].wait()
        stores.append(pltpu.make_async_copy(cells, cells_out, left.at[2, 0]))
        stores[-1].start()
        for copy in stores:
            copy.wait()

    filters = jax.ShapeDtypeStruct(wide, F32)
    grad_frames, one, two = pl.pallas_call(
        widened,
        out_shape=(jax.ShapeDtypeStruct((F, R, C, J), BF16), filters, filters),
        in_specs=[hbm] * 3,
        out_specs=(hbm,) * 3,
        scratch_shapes=[
            pltpu.VMEM((F, R, C, J), BF16), pltpu.VMEM(narrow, BF16), pltpu.VMEM(narrow, BF16),
            pltpu.VMEM(wide, F32), pltpu.VMEM(wide, F32), dma((3, 3)), dma((3, 3)),
        ],
        compiler_params=pltpu.CompilerParams(vmem_limit_bytes=56 * 1024 * 1024),
    )(grad_frames, one, two)

    def whole(grad):
        if T > 2:
            groups = [list(range(0, T, 2)), list(range(1, T, 2))]
            grad = lax.psum(grad, "tm", axis_index_groups=groups)
        return grad.reshape(3, 3, 3, C, CC).transpose(3, 0, 1, 2, 4)

    return grad_frames, whole(one), whole(two)


def solution(mesh):
    sizes = (mesh.shape["tm"], mesh.shape["height"], mesh.shape["chan"])
    cells = P("tm", "height", "chan", None)
    filters = P("chan", None, None, None, None)
    return jax.shard_map(
        functools.partial(on_device, sizes),
        mesh=mesh,
        in_specs=(cells, cells, filters, filters),
        out_specs=(cells, filters, filters),
        check_vma=False,
    )
```

```python
import functools

import jax
import jax.numpy as jnp
from jax import lax
from jax.experimental import pallas as pl
from jax.experimental.pallas import tpu as pltpu
from jax.sharding import PartitionSpec as P

BF16 = jnp.bfloat16
F32 = jnp.float32
MESH = pl.DeviceIdType.MESH
HALO = 5


def moved_cols(block, offset):
    lane = lax.broadcasted_iota(jnp.int32, block.shape, 1)
    cols = block.shape[1]
    if offset > 0:
        return jnp.where(lane == cols - 1, 0.0, pltpu.roll(block, cols - 1, 1))
    return jnp.where(lane == 0, 0.0, pltpu.roll(block, 1, 1))


def kernel(
    sizes,
    frames, gout, w1_in, w2_in,
    gf_out, g1_out, g2_out,
    w1, w2, x, g, gsh, gp, gpsh, w1t, w2t, pre, ga, gain, act, gf, gfin, via,
    town, tsend, trecv, hown, hsend, hrecv, fin,
    z_send, z_recv, zz_send, zz_recv, xh_send, xh_recv, gh_send, gh_recv,
    t_send, t_recv, h_send, h_recv, a_send, a_recv, p_send, p_recv, local,
):
    T, H, Z = sizes
    F, R, C, J = gf_out.shape
    CC = C * Z
    O = C
    slabs = F * R
    part = 3 * O // H
    FAR = 3 if Z == 4 else Z
    tm, h, z = lax.axis_index("tm"), lax.axis_index("height"), lax.axis_index("chan")
    pair = tm + 1 - 2 * lax.rem(tm, 2)
    parity = lax.rem(tm, 2)

    up, down = h > 0, h < H - 1
    has_prev, has_next = tm > 0, tm < T - 1

    def zpeer(d):
        return {"chan": lax.rem(z + d, Z)}

    def hpeer(d):
        return {"height": lax.rem(h + d, H)}

    both = jnp.logical_and

    loads = [
        pltpu.make_async_copy(w2_in, w2, local.at[0]),
        pltpu.make_async_copy(w1_in, w1, local.at[1]),
        pltpu.make_async_copy(
            frames,
            x.at[pl.ds(F, F), pl.ds(1, R), pl.ds(pl.multiple_of(z * C, C), C), :],
            local.at[4],
        ),
        pltpu.make_async_copy(gout, g.at[pl.ds(0, F), pl.ds(1, R)], local.at[5]),
    ]
    for k in (2, 3, 0, 1):
        loads[k].start()

    barrier = pltpu.get_barrier_semaphore()
    for d in range(1, Z):
        pl.semaphore_signal(barrier, inc=1, device_id=zpeer(d), device_id_type=MESH)
    for d in range(1, H):
        pl.semaphore_signal(barrier, inc=1, device_id=hpeer(d), device_id_type=MESH)
    for cond_t, dt in ((has_prev, -1), (has_next, 1)):
        @pl.when(cond_t)
        def _(dt=dt):
            pl.semaphore_signal(barrier, inc=1, device_id={"tm": tm + dt}, device_id_type=MESH)
        for cond_h, dh in ((up, -1), (down, 1)):
            @pl.when(jnp.logical_and(cond_t, cond_h))
            def _(dt=dt, dh=dh):
                pl.semaphore_signal(
                    barrier, inc=1, device_id={"tm": tm + dt, "height": h + dh}, device_id_type=MESH
                )
    def near(p):
        return both(z != p, jnp.abs(z - p) < FAR)

    def zero_edges(ext, dt):
        f0 = 0 if dt > 0 else F

        @pl.when(jnp.logical_not(has_prev if dt > 0 else has_next))
        def _():
            ext[f0 : f0 + F] = jnp.zeros((F,) + ext.shape[1:], ext.dtype)

        @pl.when(jnp.logical_not(up))
        def _():
            ext[:, 0] = jnp.zeros((2 * F,) + ext.shape[2:], ext.dtype)

        @pl.when(jnp.logical_not(down))
        def _():
            ext[:, R + 1] = jnp.zeros((2 * F,) + ext.shape[2:], ext.dtype)

    zero_edges(g, -1)
    zero_edges(gp, -1)
    zero_edges(x, 1)
    for dst in (gain, gfin):
        for q in range(Z):
            @pl.when(jnp.logical_not(near(q)))
            def _(dst=dst, q=q):
                dst[q] = jnp.zeros(dst.shape[1:], dst.dtype)

    def turned(weight, out):
        flat = weight[...].reshape(27 * O, CC)
        for k in range(0, 27 * O, 2 * J):
            end = min(k + 2 * J, 27 * O)
            out[:, k:end] = flat[k:end].T

    loads[0].wait()
    turned(w2, w2t)

    n_t = jnp.where(has_prev, 1, 0) + jnp.where(has_next, 1, 0)
    n_h = jnp.where(up, 1, 0) + jnp.where(down, 1, 0)
    pl.semaphore_wait(barrier, (Z - 1) + (H - 1) + n_t + n_t * n_h)

    pending = []

    def remote(src, dst, ssem, rsem, dev):
        return pltpu.make_async_remote_copy(
            src_ref=src, dst_ref=dst, send_sem=ssem, recv_sem=rsem, device_id=dev, device_id_type=MESH
        )

    def send(copy):
        copy.start()
        pending.append((None, copy))
        return copy

    def settle(sent):
        for go, copy in sent:
            if go is None:
                copy.wait_send()
            else:
                pl.when(go)(copy.wait_send)

    def send_if(go, copy):
        pl.when(go)(copy.start)
        pending.append((go, copy))

    def halo_plan(ext, dt, chan_slice, ssems, rsems):
        o0, f0 = (F, 0) if dt > 0 else (0, F)
        to_t = has_next if dt > 0 else has_prev
        from_t = has_prev if dt > 0 else has_next

        def at(frame, row, rows):
            return ext.at[pl.ds(frame, F), pl.ds(row, rows), chan_slice, :]

        plan = [
            (to_t, from_t, at(o0, 1, R), at(f0, 1, R), {"tm": tm + dt}),
            (down, up, at(o0, R, 1), at(o0, 0, 1), {"height": h + 1}),
            (up, down, at(o0, 1, 1), at(o0, R + 1, 1), {"height": h - 1}),
            (
                both(to_t, down), both(from_t, up),
                at(o0, R, 1), at(f0, 0, 1), {"tm": tm + dt, "height": h + 1},
            ),
            (
                both(to_t, up), both(from_t, down),
                at(o0, 1, 1), at(f0, R + 1, 1), {"tm": tm + dt, "height": h - 1},
            ),
        ]
        return [
            (go, come, remote(src, dst, ssems.at[k], rsems.at[k], dev))
            for k, (go, come, src, dst, dev) in enumerate(plan)
        ]

    def depart(plan):
        for go, _, copy in plan:
            pl.when(go)(copy.start)

    def arrive(plan):
        for _, come, copy in plan:
            pl.when(come)(copy.wait_recv)

    def chunk(index):
        return pl.ds(pl.multiple_of(index * C, C), C)

    mine = chunk(z)

    def gather(phase, block):
        for p in sorted(range(Z), key=lambda p: abs(2 * p - Z + 1)):
            send_if(near(p), remote(
                block(z), block(z), z_send.at[phase, p], z_recv.at[phase, z], {"chan": p}
            ))

    def nearest(k):
        low = z < Z // 2
        side = jnp.where(low, z, Z - 1 - z)
        other = jnp.where(k < side, k, k + 1)
        return jnp.where(low, other, Z - 1 - other)

    def gathered(phase, k, block, unless=None):
        q = nearest(k)
        landed = remote(
            block(q), block(q), z_send.at[phase, q], z_recv.at[phase, q], zpeer(1)
        )
        if unless is None:
            landed.wait_recv()
        else:
            pl.when(jnp.logical_not(unless))(landed.wait_recv)
        if FAR < Z and unless is None:
            for go, dz in (
                (both(both(q < z, z < Z - 1), z + 1 - q >= FAR), 1),
                (both(both(q > z, z > 0), q + 1 - z >= FAR), -1),
            ):
                send_if(go, remote(
                    block(q), block(q), zz_send.at[phase, k], z_recv.at[phase, q], {"chan": z + dz}
                ))
        return q

    middle = both(z > 0, z < Z - 1)

    def forwarded(phase, block):
        if FAR < Z:
            q = nearest(Z - 2)

            @pl.when(middle)
            def _():
                remote(
                    block(q), block(q), z_send.at[phase, q], z_recv.at[phase, q], zpeer(1)
                ).wait_recv()

            for go, dz in ((both(middle, q < z), 1), (both(middle, q > z), -1)):
                send_if(go, remote(
                    block(q), block(q), zz_send.at[phase, 0], z_recv.at[phase, q], {"chan": z + dz}
                ))

    ends = (0, Z - 1) if FAR < Z else ()

    def takes(p):
        return z == (1 if p == Z - 1 else Z - 2)

    def passed(phase, src, p):
        dz = 1 if p == Z - 1 else -1
        return remote(
            src.at[:, pl.ds(p * C, C), :], via.at[phase // 2],
            zz_send.at[phase, 0], zz_recv.at[phase], {"chan": lax.rem(z + dz + Z, Z)},
        )

    def direct(phase, src, dst, p):
        return remote(
            src.at[:, pl.ds(p * C, C), :], dst.at[z], z_send.at[phase, p], z_recv.at[phase, z], {"chan": p}
        )

    def scatter(phase, src, dst, only=None):
        for p in ends:
            if only is not middle:
                send_if(z == Z - 1 - p, passed(phase, src, p))
        for p in range(Z):
            go = both(near(p), jnp.logical_not(takes(p))) if p in ends else near(p)
            go = go if only is None else both(go, only)
            pl.when(go)(direct(phase, src, dst, p).start)

    def scatter_rest(phase, src, dst):
        for p in ends:
            @pl.when(takes(p))
            def _(p=p):
                passed(phase, src, p).wait_recv()
                rows = slice(p * C, p * C + C)
                src[:, rows, :] = (
                    src[:, rows, :].astype(F32) + via[phase // 2].astype(F32)
                ).astype(BF16)
                direct(phase, src, dst, p).start()
        for p in range(Z):
            pending.append((near(p), direct(phase, src, dst, p)))

    def scattered(phase, src, dst):
        for q in range(Z):
            pl.when(near(q))(remote(
                src.at[:, pl.ds(0, C), :], dst.at[q], z_send.at[phase, q], z_recv.at[phase, q], zpeer(1)
            ).wait_recv)

    def summed(src, dst, s):
        total = src[s, mine, :].astype(F32)
        for q in range(Z):
            total += dst[q, s].astype(F32)
        return total

    def x_block(q):
        return x.at[pl.ds(F, F), pl.ds(1, R), chunk(q), :]

    def act_block(q):
        return act.at[:, chunk(q), :]

    def x_halo(q):
        return halo_plan(x, 1, chunk(q), xh_send.at[q], xh_recv.at[q])

    loads[2].wait()
    gather(0, x_block)
    loads[3].wait()
    g_plan = halo_plan(g, -1, pl.ds(0, C), gh_send.at[0], gh_recv.at[0])
    depart(g_plan)
    depart(x_halo(z))

    def spread(src, dst, t, i):
        wide = src[t, i].astype(F32)
        dst[t, i, 0:O] = moved_cols(wide, 1).astype(BF16)
        dst[t, i, O : 2 * O] = src[t, i]
        dst[t, i, 2 * O : 3 * O] = moved_cols(wide, -1).astype(BF16)

    def back(source, weight, out, start=0, stop=slabs // 2):
        @pl.loop(start, stop)
        def _(s):
            t, i = s // (R // 2), 2 * lax.rem(s, R // 2)
            windows = [
                jnp.concatenate([source[t + 2 - a, i + 2 - b], source[t + 2 - a, i + 3 - b]], 1)
                for a in range(3)
                for b in range(3)
            ]
            total = jnp.dot(weight[...], jnp.concatenate(windows, 0), preferred_element_type=F32)
            out[2 * s] = total[:, :J].astype(BF16)
            out[2 * s + 1] = total[:, J:].astype(BF16)

    arrive(g_plan)

    @pl.loop(0, 2 * F * (R + 2), unroll=4)
    def _(s):
        spread(g, gsh, s // (R + 2), lax.rem(s, R + 2))

    depart(x_halo(gathered(0, 0, x_block)))
    back(gsh, w2t, ga, 0, slabs // 4)
    if Z > 2:
        depart(x_halo(gathered(0, 1, x_block)))
    back(gsh, w2t, ga, slabs // 4, slabs // 2)
    scatter(1, ga, gain)
    loads[1].wait()

    for k in range(2, Z - 1):
        depart(x_halo(gathered(0, k, x_block)))
    scatter_rest(1, ga, gain)

    turned(w1, w1t)

    for q in range(Z):
        arrive(x_halo(q))

    @pl.loop(0, slabs // 2)
    def _(s):
        t, i = s // (R // 2), 2 * lax.rem(s, R // 2)
        windows = [
            jnp.concatenate([x[t + a, i + b], x[t + a, i + b + 1]], 1)
            for a in range(3)
            for b in range(3)
        ]
        taps_of = jnp.concatenate([w1[ab] for ab in range(9)], 1)
        total = jnp.dot(taps_of, jnp.concatenate(windows, 0), preferred_element_type=F32)
        for half in range(2):
            cols = total[:, half * J : (half + 1) * J]
            value = moved_cols(cols[0:O], -1) + cols[O : 2 * O] + moved_cols(cols[2 * O :], 1)
            pre[2 * s + half] = value
            act[2 * s + half, mine, :] = (value * jax.nn.sigmoid(value)).astype(BF16)

    gather(2, act_block)
    scattered(1, ga, gain)

    @pl.loop(0, slabs, unroll=4)
    def _(s):
        t, i = s // R, lax.rem(s, R)
        total = summed(ga, gain, s)
        value = pre[s]
        sig = jax.nn.sigmoid(value)
        gp[t, i + 1] = (total * sig * (1.0 + value * (1.0 - sig))).astype(BF16)

    gp_plan = halo_plan(gp, -1, pl.ds(0, C), gh_send.at[1], gh_recv.at[1])
    depart(gp_plan)

    @pl.loop(0, slabs, unroll=4)
    def _(s):
        spread(gp, gpsh, s // R, lax.rem(s, R) + 1)

    nt = (((1,), (1,)), ((), ()))

    def row_of(source, t0, i0):
        return jnp.concatenate([source[t0 + s // R, i0 + s % R] for s in range(slabs)], 1)

    my_rows = pl.ds(pl.multiple_of(h * part, part), part)

    def taps(a):
        return pl.ds(3 * a, 3)

    def to_pair(f, a, values):
        for b, value in enumerate(values):
            left, right = value[:, :J], value[:, J:]
            town[f, 3 * a + b] = jnp.where(parity == 0, left, right)
            tsend[f, 3 * a + b] = jnp.where(parity == 0, right, left).astype(BF16)

        return send(remote(
            tsend.at[f, taps(a)], trecv.at[f, taps(a)], t_send.at[f, a], t_recv.at[f, a], {"tm": pair}
        ))

    def to_rows(f, a, copy):
        copy.wait_recv()

        @pl.loop(3 * a, 3 * a + 3, unroll=3)
        def _(ab):
            total = town[f, ab] + trecv[f, ab].astype(F32)
            hown[f, ab] = total
            hsend[f, ab] = total.astype(BF16)

        return [
            send(remote(
                hsend.at[f, taps(a), pl.ds(pl.multiple_of(lax.rem(h + d, H) * part, part), part), :],
                hrecv.at[f, d - 1, taps(a)],
                h_send.at[f, a, d - 1], h_recv.at[f, a, d - 1], hpeer(d),
            ))
            for d in range(1, H)
        ]

    def piece(f, a, row):
        return fin.at[f, parity, taps(a), pl.ds(pl.multiple_of(row * part, part), part), :]

    def relay(f, a, d):
        block = piece(f, a, lax.rem(h - d + H, H))
        return send(remote(block, block, p_send.at[f, a, d], p_recv.at[f, a, d], {"tm": pair}))

    def from_rows(f, a, copies):
        for copy in copies:
            copy.wait_recv()

        @pl.loop(3 * a, 3 * a + 3, unroll=3)
        def _(ab):
            total = hown[f, ab, my_rows, :]
            for d in range(1, H):
                total += hrecv[f, d - 1, ab].astype(F32)
            fin[f, parity, ab, my_rows, :] = total.astype(BF16)

        block = piece(f, a, h)
        copies = [
            send(remote(block, block, a_send.at[f, a, d - 1], a_recv.at[f, a, d - 1], hpeer(d)))
            for d in range(1, H)
        ]
        return copies, [relay(f, a, 0)]

    def to_other(f, a, state):
        copies, relays = state
        for d in range(1, H):
            copies[d - 1].wait_recv()
            relays.append(relay(f, a, d))
        return relays

    def first_taps(a):
        left = row_of(gpsh, 0, 1)
        return [
            lax.dot_general(left, row_of(x, a, b), nt, preferred_element_type=F32) for b in range(3)
        ]

    def second_taps(a):
        left = jnp.concatenate([row_of(gsh, 2 - a, 2 - b) for b in range(3)], 0)
        right = jnp.concatenate([act[s] for s in range(slabs)], 1)
        value = lax.dot_general(left, right, nt, preferred_element_type=F32)
        return [value[b * 3 * O : (b + 1) * 3 * O] for b in range(3)]

    def staggered(f, taps_of):
        copies = [to_pair(f, 0, taps_of(0))]
        rows = []
        for a in range(1, 3):
            copies.append(to_pair(f, a, taps_of(a)))
            rows.append(to_rows(f, a - 1, copies[a - 1]))
        rows.append(to_rows(f, 2, copies[2]))
        return rows

    one = staggered(0, first_taps)
    forwarded(2, act_block)

    arrive(gp_plan)

    @pl.loop(0, F * (R + 2), unroll=4)
    def _(s):
        spread(gp, gpsh, F + s // (R + 2), lax.rem(s, R + 2))

    for t in range(F):
        for i in (0, R + 1):
            spread(gp, gpsh, t, i)
    back(gpsh, w1t, gf)
    scatter(3, gf, gfin, only=jnp.logical_not(middle))
    one = [from_rows(0, a, one[a]) for a in range(3)]

    for k in range(Z - 1):
        gathered(2, k, act_block, unless=both(middle, k == Z - 2) if FAR < Z else both(z < 0, z > 0))
    scatter(3, gf, gfin, only=middle)

    drained = len(pending)
    two = staggered(1, second_taps)
    one = [to_other(0, a, one[a]) for a in range(3)]
    scatter_rest(3, gf, gfin)
    two = [from_rows(1, a, two[a]) for a in range(3)]
    settle(pending[:drained])
    for plan in [g_plan, gp_plan] + [x_halo(q) for q in range(Z)]:
        settle([(go, copy) for go, _, copy in plan])

    stores = []

    def store(f, a, relays, out):
        for copy in relays:
            copy.wait_recv()
        copy = pltpu.make_async_copy(fin.at[f, :, taps(a)], out.at[:, taps(a)], local.at[3 * f + a])
        copy.start()
        stores.append(copy)

    for a in range(3):
        store(0, a, one[a], g1_out)
    two = [to_other(1, a, two[a]) for a in range(3)]
    scattered(3, gf, gfin)

    @pl.loop(0, slabs, unroll=4)
    def _(s):
        gf_out[s // R, lax.rem(s, R)] = summed(gf, gfin, s).astype(BF16)

    for a in range(3):
        store(1, a, two[a], g2_out)

    settle(pending[drained:])
    for copy in stores:
        copy.wait()


def on_device(sizes, frames, grad_out, weight_one, weight_two):
    T, H, Z = sizes
    F, R, C, J = frames.shape
    CC, slabs, part = C * Z, F * R, 3 * C // H

    def taps_first(weight):
        return weight.transpose(1, 2, 3, 0, 4).reshape(9, 3 * C, CC)

    dma = pltpu.SemaphoreType.DMA
    ext = (2 * F, R + 2)
    scratch = [
        pltpu.VMEM((9, 3 * C, CC), BF16),
        pltpu.VMEM((9, 3 * C, CC), BF16),
        pltpu.VMEM(ext + (CC, J), BF16),
        pltpu.VMEM(ext + (C, J), BF16),
        pltpu.VMEM(ext + (3 * C, J), BF16),
        pltpu.VMEM(ext + (C, J), BF16),
        pltpu.VMEM(ext + (3 * C, J), BF16),
        pltpu.VMEM((CC, 27 * C), BF16),
        pltpu.VMEM((CC, 27 * C), BF16),
        pltpu.VMEM((slabs, C, J), F32),
        pltpu.VMEM((slabs, CC, J), BF16),
        pltpu.VMEM((Z, slabs, C, J), BF16),
        pltpu.VMEM((slabs, CC, J), BF16),
        pltpu.VMEM((slabs, CC, J), BF16),
        pltpu.VMEM((Z, slabs, C, J), BF16),
        pltpu.VMEM((2, slabs, C, J), BF16),
        pltpu.VMEM((2, 9, 3 * C, CC // 2), F32),
        pltpu.VMEM((2, 9, 3 * C, CC // 2), BF16),
        pltpu.VMEM((2, 9, 3 * C, CC // 2), BF16),
        pltpu.VMEM((2, 9, 3 * C, CC // 2), F32),
        pltpu.VMEM((2, 9, 3 * C, CC // 2), BF16),
        pltpu.VMEM((2, H - 1, 9, part, CC // 2), BF16),
        pltpu.VMEM((2, 2, 9, 3 * C, CC // 2), BF16),
        dma((4, Z)), dma((4, Z)), dma((4, Z)), dma((4,)),
        dma((Z, HALO)), dma((Z, HALO)), dma((2, HALO)), dma((2, HALO)),
        dma((2, 3)), dma((2, 3)), dma((2, 3, H - 1)), dma((2, 3, H - 1)),
        dma((2, 3, H - 1)), dma((2, 3, H - 1)), dma((2, 3, H)), dma((2, 3, H)), dma((6,)),
    ]
    vmem = pl.BlockSpec(memory_space=pltpu.VMEM)
    hbm = pl.BlockSpec(memory_space=pl.ANY)
    grad_frames, one, two = pl.pallas_call(
        functools.partial(kernel, sizes),
        out_shape=(
            jax.ShapeDtypeStruct((F, R, C, J), BF16),
            jax.ShapeDtypeStruct((2, 9, 3 * C, CC // 2), BF16),
            jax.ShapeDtypeStruct((2, 9, 3 * C, CC // 2), BF16),
        ),
        in_specs=[hbm] * 4,
        out_specs=(vmem, hbm, hbm),
        scratch_shapes=scratch,
        compiler_params=pltpu.CompilerParams(
            collective_id=0, has_side_effects=True, vmem_limit_bytes=56 * 1024 * 1024
        ),
    )(frames, grad_out, taps_first(weight_one), taps_first(weight_two))

    narrow, wide = (2, 9, 3 * C, CC // 2), (9, 3 * C, CC)

    def widened(
        cells_in, one_in, two_in, cells_out, one_out, two_out,
        cells, narrow_one, narrow_two, wide_one, wide_two, arrived, left,
    ):
        both = ((one_in, narrow_one, wide_one, one_out), (two_in, narrow_two, wide_two, two_out))
        fetch = []
        for f, (source, near, _, _) in enumerate(both):
            for a in range(3):
                taps = pl.ds(3 * a, 3)
                fetch.append(pltpu.make_async_copy(source.at[:, taps], near.at[:, taps], arrived.at[f, a]))
        fetch.append(pltpu.make_async_copy(cells_in, cells, arrived.at[2, 0]))
        for copy in fetch:
            copy.start()
        stores = []
        for f, (_, near, far, out) in enumerate(both):
            for a in range(3):
                fetch[3 * f + a].wait()
                for ab in range(3 * a, 3 * a + 3):
                    for half in range(2):
                        far[ab, :, half * CC // 2 : (half + 1) * CC // 2] = near[half, ab].astype(F32)
                taps = pl.ds(3 * a, 3)
                stores.append(pltpu.make_async_copy(far.at[taps], out.at[taps], left.at[f, a]))
                stores[-1].start()
        fetch[6].wait()
        stores.append(pltpu.make_async_copy(cells, cells_out, left.at[2, 0]))
        stores[-1].start()
        for copy in stores:
            copy.wait()

    filters = jax.ShapeDtypeStruct(wide, F32)
    grad_frames, one, two = pl.pallas_call(
        widened,
        out_shape=(jax.ShapeDtypeStruct((F, R, C, J), BF16), filters, filters),
        in_specs=[hbm] * 3,
        out_specs=(hbm,) * 3,
        scratch_shapes=[
            pltpu.VMEM((F, R, C, J), BF16), pltpu.VMEM(narrow, BF16), pltpu.VMEM(narrow, BF16),
            pltpu.VMEM(wide, F32), pltpu.VMEM(wide, F32), dma((3, 3)), dma((3, 3)),
        ],
        compiler_params=pltpu.CompilerParams(vmem_limit_bytes=56 * 1024 * 1024),
    )(grad_frames, one, two)

    def whole(grad):
        if T > 2:
            groups = [list(range(0, T, 2)), list(range(1, T, 2))]
            grad = lax.psum(grad, "tm", axis_index_groups=groups)
        return grad.reshape(3, 3, 3, C, CC).transpose(3, 0, 1, 2, 4)

    return grad_frames, whole(one), whole(two)


def solution(mesh):
    sizes = (mesh.shape["tm"], mesh.shape["height"], mesh.shape["chan"])
    cells = P("tm", "height", "chan", None)
    filters = P("chan", None, None, None, None)
    return jax.shard_map(
        functools.partial(on_device, sizes),
        mesh=mesh,
        in_specs=(cells, cells, filters, filters),
        out_specs=(cells, filters, filters),
        check_vma=False,
    )
```

```python
import functools

import jax
import jax.numpy as jnp
from jax import lax
from jax.experimental import pallas as pl
from jax.experimental.pallas import tpu as pltpu
from jax.sharding import PartitionSpec as P

BF16 = jnp.bfloat16
F32 = jnp.float32
MESH = pl.DeviceIdType.MESH
HALO = 5


def moved_cols(block, offset):
    lane = lax.broadcasted_iota(jnp.int32, block.shape, 1)
    cols = block.shape[1]
    if offset > 0:
        return jnp.where(lane == cols - 1, 0.0, pltpu.roll(block, cols - 1, 1))
    return jnp.where(lane == 0, 0.0, pltpu.roll(block, 1, 1))


def kernel(
    sizes,
    frames, gout, w1_in, w2_in,
    gf_out, g1_out, g2_out,
    w1, w2, x, g, gsh, gp, gpsh, w1t, w2t, pre, ga, gain, act, gf, gfin, via,
    town, tsend, trecv, hown, hsend, hrecv, fin,
    z_send, z_recv, zz_send, zz_recv, xh_send, xh_recv, gh_send, gh_recv,
    t_send, t_recv, h_send, h_recv, a_send, a_recv, p_send, p_recv, local,
):
    T, H, Z = sizes
    F, R, C, J = gf_out.shape
    CC = C * Z
    O = C
    slabs = F * R
    part = 3 * O // H
    FAR = 3 if Z == 4 else Z
    tm, h, z = lax.axis_index("tm"), lax.axis_index("height"), lax.axis_index("chan")
    pair = tm + 1 - 2 * lax.rem(tm, 2)
    parity = lax.rem(tm, 2)

    up, down = h > 0, h < H - 1
    has_prev, has_next = tm > 0, tm < T - 1

    def zpeer(d):
        return {"chan": lax.rem(z + d, Z)}

    def hpeer(d):
        return {"height": lax.rem(h + d, H)}

    both = jnp.logical_and

    loads = [
        pltpu.make_async_copy(w2_in, w2, local.at[0]),
        pltpu.make_async_copy(w1_in, w1, local.at[1]),
        pltpu.make_async_copy(
            frames,
            x.at[pl.ds(F, F), pl.ds(1, R), pl.ds(pl.multiple_of(z * C, C), C), :],
            local.at[4],
        ),
        pltpu.make_async_copy(gout, g.at[pl.ds(0, F), pl.ds(1, R)], local.at[5]),
    ]
    for k in (2, 3, 0, 1):
        loads[k].start()

    barrier = pltpu.get_barrier_semaphore()
    for d in range(1, Z):
        pl.semaphore_signal(barrier, inc=1, device_id=zpeer(d), device_id_type=MESH)
    for d in range(1, H):
        pl.semaphore_signal(barrier, inc=1, device_id=hpeer(d), device_id_type=MESH)
    for cond_t, dt in ((has_prev, -1), (has_next, 1)):
        @pl.when(cond_t)
        def _(dt=dt):
            pl.semaphore_signal(barrier, inc=1, device_id={"tm": tm + dt}, device_id_type=MESH)
        for cond_h, dh in ((up, -1), (down, 1)):
            @pl.when(jnp.logical_and(cond_t, cond_h))
            def _(dt=dt, dh=dh):
                pl.semaphore_signal(
                    barrier, inc=1, device_id={"tm": tm + dt, "height": h + dh}, device_id_type=MESH
                )
    reach = (FAR, FAR, Z, Z)

    def near(p, phase):
        return both(z != p, jnp.abs(z - p) < reach[phase])

    def zero_edges(ext, dt):
        f0 = 0 if dt > 0 else F

        @pl.when(jnp.logical_not(has_prev if dt > 0 else has_next))
        def _():
            ext[f0 : f0 + F] = jnp.zeros((F,) + ext.shape[1:], ext.dtype)

        @pl.when(jnp.logical_not(up))
        def _():
            ext[:, 0] = jnp.zeros((2 * F,) + ext.shape[2:], ext.dtype)

        @pl.when(jnp.logical_not(down))
        def _():
            ext[:, R + 1] = jnp.zeros((2 * F,) + ext.shape[2:], ext.dtype)

    zero_edges(g, -1)
    zero_edges(gp, -1)
    zero_edges(x, 1)
    for dst, phase in ((gain, 1), (gfin, 3)):
        for q in range(Z):
            @pl.when(jnp.logical_not(near(q, phase)))
            def _(dst=dst, q=q):
                dst[q] = jnp.zeros(dst.shape[1:], dst.dtype)

    def turned(weight, out):
        flat = weight[...].reshape(27 * O, CC)
        for k in range(0, 27 * O, 2 * J):
            end = min(k + 2 * J, 27 * O)
            out[:, k:end] = flat[k:end].T

    loads[0].wait()
    turned(w2, w2t)

    n_t = jnp.where(has_prev, 1, 0) + jnp.where(has_next, 1, 0)
    n_h = jnp.where(up, 1, 0) + jnp.where(down, 1, 0)
    pl.semaphore_wait(barrier, (Z - 1) + (H - 1) + n_t + n_t * n_h)

    pending = []

    def remote(src, dst, ssem, rsem, dev):
        return pltpu.make_async_remote_copy(
            src_ref=src, dst_ref=dst, send_sem=ssem, recv_sem=rsem, device_id=dev, device_id_type=MESH
        )

    def send(copy):
        copy.start()
        pending.append((None, copy))
        return copy

    def settle(sent):
        for go, copy in sent:
            if go is None:
                copy.wait_send()
            else:
                pl.when(go)(copy.wait_send)

    def send_if(go, copy):
        pl.when(go)(copy.start)
        pending.append((go, copy))

    def halo_plan(ext, dt, chan_slice, ssems, rsems):
        o0, f0 = (F, 0) if dt > 0 else (0, F)
        to_t = has_next if dt > 0 else has_prev
        from_t = has_prev if dt > 0 else has_next

        def at(frame, row, rows):
            return ext.at[pl.ds(frame, F), pl.ds(row, rows), chan_slice, :]

        plan = [
            (to_t, from_t, at(o0, 1, R), at(f0, 1, R), {"tm": tm + dt}),
            (down, up, at(o0, R, 1), at(o0, 0, 1), {"height": h + 1}),
            (up, down, at(o0, 1, 1), at(o0, R + 1, 1), {"height": h - 1}),
            (
                both(to_t, down), both(from_t, up),
                at(o0, R, 1), at(f0, 0, 1), {"tm": tm + dt, "height": h + 1},
            ),
            (
                both(to_t, up), both(from_t, down),
                at(o0, 1, 1), at(f0, R + 1, 1), {"tm": tm + dt, "height": h - 1},
            ),
        ]
        return [
            (go, come, remote(src, dst, ssems.at[k], rsems.at[k], dev))
            for k, (go, come, src, dst, dev) in enumerate(plan)
        ]

    def depart(plan):
        for go, _, copy in plan:
            pl.when(go)(copy.start)

    def arrive(plan):
        for _, come, copy in plan:
            pl.when(come)(copy.wait_recv)

    def chunk(index):
        return pl.ds(pl.multiple_of(index * C, C), C)

    mine = chunk(z)

    def gather(phase, block):
        for p in sorted(range(Z), key=lambda p: abs(2 * p - Z + 1)):
            send_if(near(p, phase), remote(
                block(z), block(z), z_send.at[phase, p], z_recv.at[phase, z], {"chan": p}
            ))

    def nearest(k):
        low = z < Z // 2
        side = jnp.where(low, z, Z - 1 - z)
        other = jnp.where(k < side, k, k + 1)
        return jnp.where(low, other, Z - 1 - other)

    def gathered(phase, k, block, unless=None):
        q = nearest(k)
        landed = remote(
            block(q), block(q), z_send.at[phase, q], z_recv.at[phase, q], zpeer(1)
        )
        if unless is None:
            landed.wait_recv()
        else:
            pl.when(jnp.logical_not(unless))(landed.wait_recv)
        if reach[phase] < Z and unless is None:
            for go, dz in (
                (both(both(q < z, z < Z - 1), z + 1 - q >= FAR), 1),
                (both(both(q > z, z > 0), q + 1 - z >= FAR), -1),
            ):
                send_if(go, remote(
                    block(q), block(q), zz_send.at[phase, k], z_recv.at[phase, q], {"chan": z + dz}
                ))
        return q

    middle = both(z > 0, z < Z - 1)

    def forwarded(phase, block):
        if reach[phase] < Z:
            q = nearest(Z - 2)

            @pl.when(middle)
            def _():
                remote(
                    block(q), block(q), z_send.at[phase, q], z_recv.at[phase, q], zpeer(1)
                ).wait_recv()

            for go, dz in ((both(middle, q < z), 1), (both(middle, q > z), -1)):
                send_if(go, remote(
                    block(q), block(q), zz_send.at[phase, 0], z_recv.at[phase, q], {"chan": z + dz}
                ))

    def ends(phase):
        return (0, Z - 1) if reach[phase] < Z else ()

    def takes(p):
        return z == (1 if p == Z - 1 else Z - 2)

    def passed(phase, src, p):
        dz = 1 if p == Z - 1 else -1
        return remote(
            src.at[:, pl.ds(p * C, C), :], via.at[phase // 2],
            zz_send.at[phase, 0], zz_recv.at[phase], {"chan": lax.rem(z + dz + Z, Z)},
        )

    def direct(phase, src, dst, p):
        return remote(
            src.at[:, pl.ds(p * C, C), :], dst.at[z], z_send.at[phase, p], z_recv.at[phase, z], {"chan": p}
        )

    def scatter(phase, src, dst, only=None):
        for p in ends(phase):
            if only is not middle:
                send_if(z == Z - 1 - p, passed(phase, src, p))
        for p in range(Z):
            go = near(p, phase)
            go = both(go, jnp.logical_not(takes(p))) if p in ends(phase) else go
            go = go if only is None else both(go, only)
            pl.when(go)(direct(phase, src, dst, p).start)

    def scatter_rest(phase, src, dst):
        for p in ends(phase):
            @pl.when(takes(p))
            def _(p=p):
                passed(phase, src, p).wait_recv()
                rows = slice(p * C, p * C + C)
                src[:, rows, :] = (
                    src[:, rows, :].astype(F32) + via[phase // 2].astype(F32)
                ).astype(BF16)
                direct(phase, src, dst, p).start()
        for p in range(Z):
            pending.append((near(p, phase), direct(phase, src, dst, p)))

    def scattered(phase, src, dst):
        for q in range(Z):
            pl.when(near(q, phase))(remote(
                src.at[:, pl.ds(0, C), :], dst.at[q], z_send.at[phase, q], z_recv.at[phase, q], zpeer(1)
            ).wait_recv)

    def summed(src, dst, s):
        total = src[s, mine, :].astype(F32)
        for q in range(Z):
            total += dst[q, s].astype(F32)
        return total

    def x_block(q):
        return x.at[pl.ds(F, F), pl.ds(1, R), chunk(q), :]

    def act_block(q):
        return act.at[:, chunk(q), :]

    def x_halo(q):
        return halo_plan(x, 1, chunk(q), xh_send.at[q], xh_recv.at[q])

    loads[2].wait()
    gather(0, x_block)
    loads[3].wait()
    g_plan = halo_plan(g, -1, pl.ds(0, C), gh_send.at[0], gh_recv.at[0])
    depart(g_plan)
    depart(x_halo(z))

    def spread(src, dst, t, i):
        wide = src[t, i].astype(F32)
        dst[t, i, 0:O] = moved_cols(wide, 1).astype(BF16)
        dst[t, i, O : 2 * O] = src[t, i]
        dst[t, i, 2 * O : 3 * O] = moved_cols(wide, -1).astype(BF16)

    def back(source, weight, out, start=0, stop=slabs // 2):
        @pl.loop(start, stop)
        def _(s):
            t, i = s // (R // 2), 2 * lax.rem(s, R // 2)
            windows = [
                jnp.concatenate([source[t + 2 - a, i + 2 - b], source[t + 2 - a, i + 3 - b]], 1)
                for a in range(3)
                for b in range(3)
            ]
            total = jnp.dot(weight[...], jnp.concatenate(windows, 0), preferred_element_type=F32)
            out[2 * s] = total[:, :J].astype(BF16)
            out[2 * s + 1] = total[:, J:].astype(BF16)

    arrive(g_plan)

    @pl.loop(0, 2 * F * (R + 2), unroll=4)
    def _(s):
        spread(g, gsh, s // (R + 2), lax.rem(s, R + 2))

    depart(x_halo(gathered(0, 0, x_block)))
    back(gsh, w2t, ga, 0, slabs // 4)
    if Z > 2:
        depart(x_halo(gathered(0, 1, x_block)))
    back(gsh, w2t, ga, slabs // 4, slabs // 2)
    scatter(1, ga, gain)
    loads[1].wait()

    for k in range(2, Z - 1):
        depart(x_halo(gathered(0, k, x_block)))
    scatter_rest(1, ga, gain)

    turned(w1, w1t)

    for q in range(Z):
        arrive(x_halo(q))

    @pl.loop(0, slabs // 2)
    def _(s):
        t, i = s // (R // 2), 2 * lax.rem(s, R // 2)
        windows = [
            jnp.concatenate([x[t + a, i + b], x[t + a, i + b + 1]], 1)
            for a in range(3)
            for b in range(3)
        ]
        taps_of = jnp.concatenate([w1[ab] for ab in range(9)], 1)
        total = jnp.dot(taps_of, jnp.concatenate(windows, 0), preferred_element_type=F32)
        for half in range(2):
            cols = total[:, half * J : (half + 1) * J]
            value = moved_cols(cols[0:O], -1) + cols[O : 2 * O] + moved_cols(cols[2 * O :], 1)
            pre[2 * s + half] = value
            act[2 * s + half, mine, :] = (value * jax.nn.sigmoid(value)).astype(BF16)

    gather(2, act_block)
    scattered(1, ga, gain)

    @pl.loop(0, slabs, unroll=4)
    def _(s):
        t, i = s // R, lax.rem(s, R)
        total = summed(ga, gain, s)
        value = pre[s]
        sig = jax.nn.sigmoid(value)
        gp[t, i + 1] = (total * sig * (1.0 + value * (1.0 - sig))).astype(BF16)

    gp_plan = halo_plan(gp, -1, pl.ds(0, C), gh_send.at[1], gh_recv.at[1])
    depart(gp_plan)

    @pl.loop(0, slabs, unroll=4)
    def _(s):
        spread(gp, gpsh, s // R, lax.rem(s, R) + 1)

    nt = (((1,), (1,)), ((), ()))

    def row_of(source, t0, i0):
        return jnp.concatenate([source[t0 + s // R, i0 + s % R] for s in range(slabs)], 1)

    my_rows = pl.ds(pl.multiple_of(h * part, part), part)

    def taps(a):
        return pl.ds(3 * a, 3)

    def to_pair(f, a, values):
        for b, value in enumerate(values):
            left, right = value[:, :J], value[:, J:]
            town[f, 3 * a + b] = jnp.where(parity == 0, left, right)
            tsend[f, 3 * a + b] = jnp.where(parity == 0, right, left).astype(BF16)

        return send(remote(
            tsend.at[f, taps(a)], trecv.at[f, taps(a)], t_send.at[f, a], t_recv.at[f, a], {"tm": pair}
        ))

    def to_rows(f, a, copy):
        copy.wait_recv()

        @pl.loop(3 * a, 3 * a + 3, unroll=3)
        def _(ab):
            total = town[f, ab] + trecv[f, ab].astype(F32)
            hown[f, ab] = total
            hsend[f, ab] = total.astype(BF16)

        return [
            send(remote(
                hsend.at[f, taps(a), pl.ds(pl.multiple_of(lax.rem(h + d, H) * part, part), part), :],
                hrecv.at[f, d - 1, taps(a)],
                h_send.at[f, a, d - 1], h_recv.at[f, a, d - 1], hpeer(d),
            ))
            for d in range(1, H)
        ]

    def piece(f, a, row):
        return fin.at[f, parity, taps(a), pl.ds(pl.multiple_of(row * part, part), part), :]

    def relay(f, a, d):
        block = piece(f, a, lax.rem(h - d + H, H))
        return send(remote(block, block, p_send.at[f, a, d], p_recv.at[f, a, d], {"tm": pair}))

    def from_rows(f, a, copies):
        for copy in copies:
            copy.wait_recv()

        @pl.loop(3 * a, 3 * a + 3, unroll=3)
        def _(ab):
            total = hown[f, ab, my_rows, :]
            for d in range(1, H):
                total += hrecv[f, d - 1, ab].astype(F32)
            fin[f, parity, ab, my_rows, :] = total.astype(BF16)

        block = piece(f, a, h)
        copies = [
            send(remote(block, block, a_send.at[f, a, d - 1], a_recv.at[f, a, d - 1], hpeer(d)))
            for d in range(1, H)
        ]
        return copies, [relay(f, a, 0)]

    def to_other(f, a, state):
        copies, relays = state
        for d in range(1, H):
            copies[d - 1].wait_recv()
            relays.append(relay(f, a, d))
        return relays

    def first_taps(a):
        left = row_of(gpsh, 0, 1)
        return [
            lax.dot_general(left, row_of(x, a, b), nt, preferred_element_type=F32) for b in range(3)
        ]

    def second_taps(a):
        left = jnp.concatenate([row_of(gsh, 2 - a, 2 - b) for b in range(3)], 0)
        right = jnp.concatenate([act[s] for s in range(slabs)], 1)
        value = lax.dot_general(left, right, nt, preferred_element_type=F32)
        return [value[b * 3 * O : (b + 1) * 3 * O] for b in range(3)]

    def staggered(f, taps_of):
        copies = [to_pair(f, 0, taps_of(0))]
        rows = []
        for a in range(1, 3):
            copies.append(to_pair(f, a, taps_of(a)))
            rows.append(to_rows(f, a - 1, copies[a - 1]))
        rows.append(to_rows(f, 2, copies[2]))
        return rows

    one = staggered(0, first_taps)
    forwarded(2, act_block)

    arrive(gp_plan)

    @pl.loop(0, F * (R + 2), unroll=4)
    def _(s):
        spread(gp, gpsh, F + s // (R + 2), lax.rem(s, R + 2))

    for t in range(F):
        for i in (0, R + 1):
            spread(gp, gpsh, t, i)
    back(gpsh, w1t, gf)
    scatter(3, gf, gfin)
    one = [from_rows(0, a, one[a]) for a in range(3)]

    for k in range(Z - 1):
        gathered(2, k, act_block, unless=both(middle, k == Z - 2) if reach[2] < Z else None)

    drained = len(pending)
    two = staggered(1, second_taps)
    one = [to_other(0, a, one[a]) for a in range(3)]
    scatter_rest(3, gf, gfin)
    two = [from_rows(1, a, two[a]) for a in range(3)]
    settle(pending[:drained])
    for plan in [g_plan, gp_plan] + [x_halo(q) for q in range(Z)]:
        settle([(go, copy) for go, _, copy in plan])

    stores = []

    def store(f, a, relays, out):
        for copy in relays:
            copy.wait_recv()
        copy = pltpu.make_async_copy(fin.at[f, :, taps(a)], out.at[:, taps(a)], local.at[3 * f + a])
        copy.start()
        stores.append(copy)

    for a in range(3):
        store(0, a, one[a], g1_out)
    two = [to_other(1, a, two[a]) for a in range(3)]
    scattered(3, gf, gfin)

    @pl.loop(0, slabs, unroll=4)
    def _(s):
        gf_out[s // R, lax.rem(s, R)] = summed(gf, gfin, s).astype(BF16)

    for a in range(3):
        store(1, a, two[a], g2_out)

    settle(pending[drained:])
    for copy in stores:
        copy.wait()


def on_device(sizes, frames, grad_out, weight_one, weight_two):
    T, H, Z = sizes
    F, R, C, J = frames.shape
    CC, slabs, part = C * Z, F * R, 3 * C // H

    def taps_first(weight):
        return weight.transpose(1, 2, 3, 0, 4).reshape(9, 3 * C, CC)

    dma = pltpu.SemaphoreType.DMA
    ext = (2 * F, R + 2)
    scratch = [
        pltpu.VMEM((9, 3 * C, CC), BF16),
        pltpu.VMEM((9, 3 * C, CC), BF16),
        pltpu.VMEM(ext + (CC, J), BF16),
        pltpu.VMEM(ext + (C, J), BF16),
        pltpu.VMEM(ext + (3 * C, J), BF16),
        pltpu.VMEM(ext + (C, J), BF16),
        pltpu.VMEM(ext + (3 * C, J), BF16),
        pltpu.VMEM((CC, 27 * C), BF16),
        pltpu.VMEM((CC, 27 * C), BF16),
        pltpu.VMEM((slabs, C, J), F32),
        pltpu.VMEM((slabs, CC, J), BF16),
        pltpu.VMEM((Z, slabs, C, J), BF16),
        pltpu.VMEM((slabs, CC, J), BF16),
        pltpu.VMEM((slabs, CC, J), BF16),
        pltpu.VMEM((Z, slabs, C, J), BF16),
        pltpu.VMEM((2, slabs, C, J), BF16),
        pltpu.VMEM((2, 9, 3 * C, CC // 2), F32),
        pltpu.VMEM((2, 9, 3 * C, CC // 2), BF16),
        pltpu.VMEM((2, 9, 3 * C, CC // 2), BF16),
        pltpu.VMEM((2, 9, 3 * C, CC // 2), F32),
        pltpu.VMEM((2, 9, 3 * C, CC // 2), BF16),
        pltpu.VMEM((2, H - 1, 9, part, CC // 2), BF16),
        pltpu.VMEM((2, 2, 9, 3 * C, CC // 2), BF16),
        dma((4, Z)), dma((4, Z)), dma((4, Z)), dma((4,)),
        dma((Z, HALO)), dma((Z, HALO)), dma((2, HALO)), dma((2, HALO)),
        dma((2, 3)), dma((2, 3)), dma((2, 3, H - 1)), dma((2, 3, H - 1)),
        dma((2, 3, H - 1)), dma((2, 3, H - 1)), dma((2, 3, H)), dma((2, 3, H)), dma((6,)),
    ]
    vmem = pl.BlockSpec(memory_space=pltpu.VMEM)
    hbm = pl.BlockSpec(memory_space=pl.ANY)
    grad_frames, one, two = pl.pallas_call(
        functools.partial(kernel, sizes),
        out_shape=(
            jax.ShapeDtypeStruct((F, R, C, J), BF16),
            jax.ShapeDtypeStruct((2, 9, 3 * C, CC // 2), BF16),
            jax.ShapeDtypeStruct((2, 9, 3 * C, CC // 2), BF16),
        ),
        in_specs=[hbm] * 4,
        out_specs=(vmem, hbm, hbm),
        scratch_shapes=scratch,
        compiler_params=pltpu.CompilerParams(
            collective_id=0, has_side_effects=True, vmem_limit_bytes=56 * 1024 * 1024
        ),
    )(frames, grad_out, taps_first(weight_one), taps_first(weight_two))

    narrow, wide = (2, 9, 3 * C, CC // 2), (9, 3 * C, CC)

    def widened(
        cells_in, one_in, two_in, cells_out, one_out, two_out,
        cells, narrow_one, narrow_two, wide_one, wide_two, arrived, left,
    ):
        both = ((one_in, narrow_one, wide_one, one_out), (two_in, narrow_two, wide_two, two_out))
        fetch = []
        for f, (source, near, _, _) in enumerate(both):
            for a in range(3):
                taps = pl.ds(3 * a, 3)
                fetch.append(pltpu.make_async_copy(source.at[:, taps], near.at[:, taps], arrived.at[f, a]))
        fetch.append(pltpu.make_async_copy(cells_in, cells, arrived.at[2, 0]))
        for copy in fetch:
            copy.start()
        stores = []
        for f, (_, near, far, out) in enumerate(both):
            for a in range(3):
                fetch[3 * f + a].wait()
                for ab in range(3 * a, 3 * a + 3):
                    for half in range(2):
                        far[ab, :, half * CC // 2 : (half + 1) * CC // 2] = near[half, ab].astype(F32)
                taps = pl.ds(3 * a, 3)
                stores.append(pltpu.make_async_copy(far.at[taps], out.at[taps], left.at[f, a]))
                stores[-1].start()
        fetch[6].wait()
        stores.append(pltpu.make_async_copy(cells, cells_out, left.at[2, 0]))
        stores[-1].start()
        for copy in stores:
            copy.wait()

    filters = jax.ShapeDtypeStruct(wide, F32)
    grad_frames, one, two = pl.pallas_call(
        widened,
        out_shape=(jax.ShapeDtypeStruct((F, R, C, J), BF16), filters, filters),
        in_specs=[hbm] * 3,
        out_specs=(hbm,) * 3,
        scratch_shapes=[
            pltpu.VMEM((F, R, C, J), BF16), pltpu.VMEM(narrow, BF16), pltpu.VMEM(narrow, BF16),
            pltpu.VMEM(wide, F32), pltpu.VMEM(wide, F32), dma((3, 3)), dma((3, 3)),
        ],
        compiler_params=pltpu.CompilerParams(vmem_limit_bytes=56 * 1024 * 1024),
    )(grad_frames, one, two)

    def whole(grad):
        if T > 2:
            groups = [list(range(0, T, 2)), list(range(1, T, 2))]
            grad = lax.psum(grad, "tm", axis_index_groups=groups)
        return grad.reshape(3, 3, 3, C, CC).transpose(3, 0, 1, 2, 4)

    return grad_frames, whole(one), whole(two)


def solution(mesh):
    sizes = (mesh.shape["tm"], mesh.shape["height"], mesh.shape["chan"])
    cells = P("tm", "height", "chan", None)
    filters = P("chan", None, None, None, None)
    return jax.shard_map(
        functools.partial(on_device, sizes),
        mesh=mesh,
        in_specs=(cells, cells, filters, filters),
        out_specs=(cells, filters, filters),
        check_vma=False,
    )
```
